128 devices in a mesh: tmpl: 32 (over z_hi, x, y), seg: 4 (over z_lo, core).
Axes of the slice: x: 4, y: 4, z: 4 (z_hi: 2, z_lo: 2; z = z_hi * 2 + z_lo), core: 2. Of those that a mesh axis runs over, the one named last changes fastest.
Arguments:
- spectra: bfloat16 [2, 2, 32, 8, 4096], P(None, None, 'tmpl', 'seg'), may hold values from -6 to 6
- templates: bfloat16 [2, 512, 4096], P(None, 'tmpl'), may hold values from -64 to 64
- bounds: int32 [512, 15], P('tmpl'), may hold values from 64 to 4032, as said below
- trigger_owner: int32 [8192, 1], P(('tmpl', 'seg')), may hold values from 0 to 31; in each aligned block of 64 rows (0 to 63, 64 to 127, ...) at most 4 rows name the same one
- trigger_template: int32 [8192], P(('tmpl', 'seg')), may hold values from 0 to 15
- trigger_segment: int32 [8192], P(('tmpl', 'seg')), may hold values from 0 to 1
- trigger_block: int32 [8192], P(('tmpl', 'seg')), may hold values from 0 to 1
Outputs:
- network_snr: float32 [512, 32, 8, 256], P('tmpl', None, 'seg')
- loudest: float32 [512], P('tmpl')
- chisq: float32 [8192, 128], P(('tmpl', 'seg'))
The draws below stay inside these ranges and needn't reach their ends.
Inputs may be any that keep to these rules, and one draw needn't show every extreme that they name: `bounds`: each row rises; the first entry, the gaps between entries and 4096 minus the last entry are all 64 or more. `trigger_owner`: at most 4 triggers of one device name the same template shard; some device names some shard exactly 4 times.
All inputs are finite; a program needn't handle non-finite values.
Results may differ from the reference program's by a relative error of at most 0.0031.
Values may be sent and summed in bfloat16 or wider, within the bound.
A program may use at most 64 MiB of HBM per device.

```python
import math
import jax
import jax.numpy as jnp
import numpy as np
from jax import lax

TMPL_DEV = 16
TEMPLATES = 512
SEG_DEV = 2
SPAN = 32
SEGROWS = 8
DET = 2
F = 4096
F0 = 10240
NSAMP = 2097152
STRIDE = 512
TIME = 256
TB = 128
NBLK = 2
NBINS = 16
MINW = 64
TRIG_DEV = 64
TRIGGERS = 8192
CAP = 4
N_TMPL = 32
N_SEG = 4


def draw_templates(key, part):
    key = jax.random.fold_in(key, 11)
    keys = jax.random.split(key, 4)
    row_scale = jnp.exp(jax.random.uniform(keys[0], (1, TEMPLATES, 1), jnp.float32) * math.log(10.0))
    col_scale = jnp.exp(jax.random.uniform(keys[1], (1, 1, F), jnp.float32) * math.log(10.0))
    values = jax.random.normal(keys[3], (2, TEMPLATES, F), jnp.float32) * row_scale * col_scale * 0.1
    return values.astype(jnp.bfloat16)


def draw_bounds(key, part):
    key = jax.random.fold_in(key, 23)
    keys = jax.random.split(key, 3)
    spare = F - NBINS * MINW
    cuts = jax.random.randint(keys[0], (TEMPLATES, NBINS - 1), 0, spare + 1, jnp.int32)
    low_row = jax.random.randint(keys[1], (), 0, TEMPLATES, jnp.int32)
    high_row = jax.random.randint(keys[2], (), 0, TEMPLATES, jnp.int32)
    rows = jnp.arange(TEMPLATES, dtype=jnp.int32)[:, None]
    columns = jnp.arange(NBINS - 1, dtype=jnp.int32)[None, :]
    cuts = jnp.where((rows == low_row) & (columns == 0), 0, cuts)
    cuts = jnp.where((rows == high_row) & (columns == NBINS - 2), spare, cuts)
    cuts = jnp.sort(cuts, axis=1)
    return (cuts + (columns + 1) * MINW).astype(jnp.int32)


def plant(result, own_key, smallest, largest):
    longest = result.shape.index(max(result.shape))
    spots = []
    for shift in (0, 1):
        where = [jax.random.randint(jax.random.fold_in(own_key, axis), (), 0, length) for axis, length in enumerate(result.shape)]
        where[longest] = (where[longest] + shift) % result.shape[longest]
        spots.append(tuple(where))
    return result.at[spots[0]].set(smallest).at[spots[1]].set(largest)


def steps_of(stream_key, shape, pieces, smallest, high):
    loudness, own = 1.0, jax.random.fold_in(stream_key, 6)
    for axis_at, blocks in pieces:
        heights = jnp.exp(jax.random.uniform(jax.random.fold_in(own, axis_at), (blocks,), jnp.float32, smallest / len(pieces), high / len(pieces)))
        loudness = loudness * jnp.repeat(heights, shape[axis_at] // blocks).reshape([-1 if axis == axis_at else 1 for axis in range(len(shape))])
    return loudness


def shared_out(own_key, own, number, rows, number_of, top, reach, slope):
    sequence = jax.random.permutation(own_key, number_of)
    packed, ordinary = load_shares(number_of, rows * top, reach, slope, True), load_shares(number_of, rows * top, reach, slope, False)
    places = jnp.arange(number_of)

    def named(sizes, rotation):
        used = int((sizes > 0).sum())
        fixed = max(1, used // 4)
        shifted = fixed + (places - fixed + rotation * (used - fixed)) % max(1, number_of - fixed)
        return jnp.zeros((number_of,), jnp.int32).at[sequence[jnp.where(places < fixed, places, shifted)]].set(jnp.asarray(sizes, jnp.int32))

    sizes = jnp.where(number % 4 == 0, named(packed, number // 4), named(ordinary, number - number // 4 - 1))
    mixed = jax.random.permutation(jax.random.fold_in(own, 3), number_of)
    giver, taker = mixed[0:number_of // 2 * 2:2], mixed[1:number_of // 2 * 2:2]
    slack = jnp.minimum(sizes[giver] - 1, reach - sizes[taker]) // 2
    slack = jnp.where((giver == sequence[0]) | (taker == sequence[0]) | (sizes[taker] == 0), 0, jnp.maximum(slack, 0))
    shifted = jax.random.randint(jax.random.fold_in(own, 4), (number_of // 2,), 0, 1 << 20) % (slack + 1)
    sizes = sizes.at[giver].add(-shifted).at[taker].add(shifted)
    labels = jnp.searchsorted(jnp.cumsum(sizes), jnp.arange(rows * top), side="right").astype(jnp.int32)
    listing = labels.reshape(top, rows).T
    listing = listing[jax.random.permutation(jax.random.fold_in(own, 1), rows)]
    rotation = jax.random.randint(jax.random.fold_in(own, 2), (rows, 1), 0, top)
    return jnp.take_along_axis(listing, (jnp.arange(top)[None, :] + rotation) % top, axis=1)


def load_shares(amount, total, bound, lean, full):
    portions = [(1 << 20) // math.isqrt(standing ** lean) + 1 for standing in range(1, amount + 1)]
    largest = bound if full else min(bound, max(-(-total // amount), total * portions[0] // sum(portions)))
    least = 1 if total - largest >= amount - 1 else 0
    holding, surplus = [largest] + [least] * (amount - 1), total - largest - least * (amount - 1)
    while surplus > 0:
        candidates = [i for i in range(1, amount) if holding[i] < largest] or [i for i in range(1, amount) if holding[i] < bound]
        mass, left = sum([portions[i] for i in candidates]), surplus
        for i in candidates:
            more = min(bound - holding[i], max(1, left * portions[i] // mass), surplus)
            holding[i] = holding[i] + more
            surplus = surplus - more
    return np.array(holding)


def normal_values(rng, extent, spread, limit, pieces=(), held_as=jnp.bfloat16):
    array = spread * jax.random.normal(rng, extent, jnp.float32)
    if pieces:
        array = array * steps_of(rng, extent, pieces, -0.22, 0.18)
    return jnp.clip(array, -limit, limit).astype(held_as)


def setup_inputs(seed: int = 0) -> dict:
    arg_keys = jax.random.split(jax.random.key(seed), 8)
    spectra = normal_values(arg_keys[0], (2, DET, SPAN, SEGROWS, F), 1.0, 6.0, ((2, 32), (3, 4)))
    templates = draw_templates(jax.random.fold_in(arg_keys[7], 71), 0)
    bounds = draw_bounds(jax.random.fold_in(arg_keys[7], 71), 0)
    trigger_owner_keys = jax.random.split(jax.random.fold_in(arg_keys[3], 1), TRIGGERS // TRIG_DEV)
    trigger_owner_turns = jax.random.permutation(jax.random.fold_in(arg_keys[3], 3), TRIGGERS // TRIG_DEV)
    trigger_owner = jax.vmap(lambda own, number: shared_out(jax.random.fold_in(arg_keys[3], 2), own, number, TRIG_DEV, N_TMPL, 1, CAP, 2))(trigger_owner_keys, trigger_owner_turns).reshape((TRIGGERS, 1))
    trigger_template = plant(jax.random.randint(arg_keys[4], (TRIGGERS,), 0, TMPL_DEV), jax.random.fold_in(arg_keys[4], 1), 0, TMPL_DEV - 1).astype(jnp.int32)
    trigger_segment = plant(jax.random.randint(arg_keys[5], (TRIGGERS,), 0, SEG_DEV), jax.random.fold_in(arg_keys[5], 1), 0, SEG_DEV - 1).astype(jnp.int32)
    trigger_block = plant(jax.random.randint(arg_keys[6], (TRIGGERS,), 0, NBLK), jax.random.fold_in(arg_keys[6], 1), 0, NBLK - 1).astype(jnp.int32)
    return {"spectra": spectra, "templates": templates, "bounds": bounds, "trigger_owner": trigger_owner, "trigger_template": trigger_template, "trigger_segment": trigger_segment, "trigger_block": trigger_block}


TWO_PI = 2.0 * math.pi
EPSILON = 1e-6


def wave_table(first_bin, bin_count, time_count):
    freq_bins = first_bin + jnp.arange(bin_count, dtype=jnp.int32)[:, None]
    time_steps = jnp.arange(time_count, dtype=jnp.int32)[None, :]
    turn_count = ((freq_bins * time_steps) % (NSAMP // STRIDE)) * STRIDE
    angles = turn_count.astype(jnp.float32) * (TWO_PI / NSAMP)
    return jnp.cos(angles).astype(jnp.bfloat16), jnp.sin(angles).astype(jnp.bfloat16)


def band_split(tmpl_rows, bin_edges):
    freq_bins = jnp.arange(tmpl_rows.shape[-1], dtype=jnp.int32)
    bin_index = jnp.sum((bin_edges[:, :, None] <= freq_bins[None, None, :]).astype(jnp.int32), axis=1)
    bin_mask = bin_index[:, None, :] == jnp.arange(NBINS, dtype=jnp.int32)[None, :, None]
    energy = tmpl_rows[:, 0] * tmpl_rows[:, 0] + tmpl_rows[:, 1] * tmpl_rows[:, 1]
    band_power = jnp.sum(jnp.where(bin_mask, energy[:, None, :], 0.0), axis=2) + EPSILON
    return band_power, bin_mask


def chi_square(seg_rows, tmpl_rows, bin_edges, blocks, cos_tb, sin_tb):
    band_power, bin_mask = band_split(tmpl_rows, bin_edges)
    total_power = jnp.sum(band_power, axis=1, keepdims=True)
    freq_bins = F0 + jnp.arange(tmpl_rows.shape[-1], dtype=jnp.int32)
    block_shift = blocks * cos_tb.shape[1]
    turn_count = ((freq_bins[None, :] * block_shift[:, None]) % (NSAMP // STRIDE)) * STRIDE
    angles = turn_count.astype(jnp.float32) * (TWO_PI / NSAMP)
    rot_cos = jnp.cos(angles)[:, None, :]
    rot_sin = jnp.sin(angles)[:, None, :]
    prod_re = seg_rows[:, 0] * tmpl_rows[:, 0][:, None, :] + seg_rows[:, 1] * tmpl_rows[:, 1][:, None, :]
    prod_im = seg_rows[:, 1] * tmpl_rows[:, 0][:, None, :] - seg_rows[:, 0] * tmpl_rows[:, 1][:, None, :]
    turned_re = (prod_re * rot_cos - prod_im * rot_sin).astype(jnp.bfloat16)
    turned_im = (prod_re * rot_sin + prod_im * rot_cos).astype(jnp.bfloat16)
    band_mask = bin_mask.astype(jnp.bfloat16)[:, :, None, :]
    left_re = turned_re[:, None] * band_mask
    left_im = turned_im[:, None] * band_mask
    corr_re = jnp.dot(left_re, cos_tb, preferred_element_type=jnp.float32) - jnp.dot(left_im, sin_tb, preferred_element_type=jnp.float32)
    corr_im = jnp.dot(left_re, sin_tb, preferred_element_type=jnp.float32) + jnp.dot(left_im, cos_tb, preferred_element_type=jnp.float32)
    whole_re = jnp.sum(corr_re, axis=1, keepdims=True)
    whole_im = jnp.sum(corr_im, axis=1, keepdims=True)
    weight = (band_power / total_power)[:, :, None, None]
    diff_re = corr_re - weight * whole_re
    diff_im = corr_im - weight * whole_im
    terms = (diff_re * diff_re + diff_im * diff_im) / band_power[:, :, None, None]
    return jnp.sum(terms, axis=(1, 2)) / (2.0 * (NBINS - 1))


def reference(spectra, templates, bounds, trigger_owner, trigger_template, trigger_segment, trigger_block):
    cos_full, sin_full = wave_table(F0, F, TIME)
    cos_tb = cos_full[:, :TB]
    sin_tb = sin_full[:, :TB]
    tmpl_rows = jnp.moveaxis(templates.astype(jnp.float32), 1, 0)
    band_power, unused_mask = band_split(tmpl_rows, bounds)
    total_power = jnp.sum(band_power, axis=1)
    spectra_f32 = spectra.astype(jnp.float32)

    def per_template(inputs):
        tmpl_one, power_one = inputs
        prod_re = (spectra_f32[0] * tmpl_one[0] + spectra_f32[1] * tmpl_one[1]).astype(jnp.bfloat16)
        prod_im = (spectra_f32[1] * tmpl_one[0] - spectra_f32[0] * tmpl_one[1]).astype(jnp.bfloat16)
        corr_re = jnp.dot(prod_re, cos_full, preferred_element_type=jnp.float32) - jnp.dot(prod_im, sin_full, preferred_element_type=jnp.float32)
        corr_im = jnp.dot(prod_re, sin_full, preferred_element_type=jnp.float32) + jnp.dot(prod_im, cos_full, preferred_element_type=jnp.float32)
        return jnp.sum(corr_re * corr_re + corr_im * corr_im, axis=0) / power_one

    network_snr = lax.map(per_template, (tmpl_rows, total_power))
    loudest = jnp.max(network_snr, axis=(1, 2, 3))

    devices = N_TMPL * N_SEG
    owners = trigger_owner[:, 0]
    source = jnp.arange(TRIGGERS, dtype=jnp.int32) // TRIG_DEV
    span_index = source // N_SEG
    row_index = (source % N_SEG) * SEG_DEV + trigger_segment
    tmpl_index = owners * TMPL_DEV + trigger_template

    def per_source(inputs):
        span_rows, seg_index, tmpl_ids, blocks = inputs
        seg_rows = jnp.moveaxis(spectra_f32[:, :, span_rows, seg_index], 2, 0)
        return chi_square(seg_rows, tmpl_rows[tmpl_ids], bounds[tmpl_ids], blocks, cos_tb, sin_tb)

    shaped = (span_index.reshape(devices, TRIG_DEV), row_index.reshape(devices, TRIG_DEV),
              tmpl_index.reshape(devices, TRIG_DEV), trigger_block.reshape(devices, TRIG_DEV))
    chisq = lax.map(per_source, shaped).reshape(TRIGGERS, TB)
    return network_snr, loudest, chisq
```

```python
import math

import jax
import jax.numpy as jnp
import numpy as np
from jax import lax
from jax.experimental import pallas as pl
from jax.experimental.pallas import tpu as pltpu
from jax.sharding import PartitionSpec as P

F = 4096
NT = 16
NBINS = 16
EPSILON = 1e-06
BF = jnp.bfloat16
F32 = jnp.float32
I32 = jnp.int32
MESH = pl.DeviceIdType.MESH
ROWS_A = 144
ROWS = 272


def tables():
    step = 2.0 * math.pi / 4096.0
    phi = np.arange(4096, dtype=np.float64) - 2048.0
    half = np.arange(128, dtype=np.float64) + 0.5
    ang = step * phi[:, None] * half[None, :]
    main = np.concatenate([np.cos(ang), np.sin(ang)], 1)
    turn = (step * 127.5 * phi).reshape(32, 128)
    rot = np.stack([np.cos(turn), np.sin(turn)])
    near = step * np.arange(128.0)[:, None] * half[None, :]
    w0 = np.concatenate(
        [
            np.concatenate([np.cos(near), np.sin(near)], 1),
            np.concatenate([-np.sin(near), np.cos(near)], 1),
        ],
        0,
    )
    far = step * (128.0 * np.arange(32.0) - 2048.0)[:, None] * half[None, :]
    far = np.stack([np.cos(far), np.sin(far)])
    return (
        jnp.asarray(main, F32).astype(BF),
        jnp.asarray(rot, F32),
        jnp.asarray(w0, F32).astype(BF),
        jnp.asarray(far, F32).astype(BF),
    )


def iota(shape, dim):
    return lax.broadcasted_iota(I32, shape, dim)


def gather_kernel(block_ref, out_ref, send_sem, recv_sem, own_sem):
    me = lax.axis_index("tmpl")
    seg = lax.axis_index("seg")
    z, x, y = me // 16, (me // 4) % 4, me % 4

    def dev(zz, xx, yy):
        return zz * 16 + ((xx + 4) % 4) * 4 + (yy + 4) % 4

    peers = [dev(1 - z, x, y), dev(z, x + 1, y), dev(z, x - 1, y), dev(z, x, y + 1), dev(z, x, y - 1)]
    barrier = pltpu.get_barrier_semaphore()
    for peer in peers:
        pl.semaphore_signal(barrier, inc=1, device_id=(peer, seg), device_id_type=MESH)
    pl.semaphore_wait(barrier, 5)

    cuts = ((0, ROWS_A), (ROWS_A, ROWS - ROWS_A))
    started = [0, 0]
    copies = []

    def part(ref, half):
        return ref.at[pl.ds(cuts[half][0], cuts[half][1])]

    def send(half, source, peer, own=False):
        src = block_ref if own else out_ref.at[source]
        copy = pltpu.make_async_remote_copy(
            src_ref=part(src, half),
            dst_ref=part(out_ref.at[source], half),
            send_sem=send_sem.at[half, started[half]],
            recv_sem=recv_sem.at[half, source],
            device_id=(peer, seg),
            device_id_type=MESH,
        )
        started[half] += 1
        copy.start()
        copies.append(copy)

    def arrived(half, source):
        pltpu.make_async_remote_copy(
            src_ref=part(out_ref.at[source], half),
            dst_ref=part(out_ref.at[source], half),
            send_sem=send_sem.at[half, 0],
            recv_sem=recv_sem.at[half, source],
            device_id=(peers[0], seg),
            device_id_type=MESH,
        ).wait_recv()

    own = pltpu.make_async_copy(block_ref, out_ref.at[me], own_sem)
    own.start()

    def near(half, zz, step):
        return dev(zz, x + step, y) if half == 0 else dev(zz, x, y + step)

    def far(half, step):
        return dev(z, x, y + step) if half == 0 else dev(z, x + step, y)

    def fan(half, source, own=False):
        for step in (1, -1):
            send(half, source, far(half, step), own)

    for half in (0, 1):
        send(half, me, peers[0], True)
        for step in (1, -1):
            send(half, me, near(half, z, step), True)
    for half in (0, 1):
        fan(half, me, True)
    mate = peers[0]
    for half in (0, 1):
        arrived(half, mate)
        for step in (1, -1):
            send(half, mate, near(half, z, step))
        fan(half, mate)
    for same in (True, False):
        for step in (1, -1):
            for half in (0, 1):
                zz = z if same else 1 - z
                source = near(half, zz, step)
                arrived(half, source)
                if (same and step == 1) or (not same and step == -1):
                    send(half, source, near(half, z, -step))
                fan(half, source)
    for same in (True, False):
        for half in (0, 1):
            source = near(half, z if same else 1 - z, 2)
            arrived(half, source)
            fan(half, source)
    order = [(True, 0), (False, 0), (True, 1), (True, -1), (False, 1), (False, -1), (True, 2), (False, 2)]

    def cross(half, same, one, two):
        zz = z if same else 1 - z
        return dev(zz, x + one, y + two) if half == 0 else dev(zz, x + two, y + one)

    for n, (same, one) in enumerate(order):
        for two in (1, -1):
            for half in (0, 1):
                source = cross(half, same, one, two)
                arrived(half, source)
                if two == (1 if n % 2 == 0 else -1):
                    send(half, source, far(half, -two))
    for same, one in order:
        for half in (0, 1):
            arrived(half, cross(half, same, one, 2))
    own.wait()
    for copy in copies:
        copy.wait_send()


def gather(block):
    return pl.pallas_call(
        gather_kernel,
        out_shape=jax.ShapeDtypeStruct((32, ROWS, 128), BF),
        in_specs=[pl.BlockSpec(memory_space=pl.ANY)],
        out_specs=pl.BlockSpec(memory_space=pl.ANY),
        scratch_shapes=[
            pltpu.SemaphoreType.DMA((2, 31)),
            pltpu.SemaphoreType.DMA((2, 32)),
            pltpu.SemaphoreType.DMA,
        ],
        compiler_params=pltpu.CompilerParams(collective_id=0, has_side_effects=True),
        name="gather",
    )(block)


def prepare(tm_ref, bounds_ref, tmf, itp, masks, pick, weight):
    lane = iota((16, 128), 1)
    sub = iota((16, 128), 0)
    quarter, chunk = lane // 32, lane % 32
    cls = sub % 3
    nat = iota((32, 128), 0) * 128 + iota((32, 128), 1)
    freq = iota((16, F), 1)
    h0 = tm_ref[0].astype(F32)
    h1 = tm_ref[1].astype(F32)
    tmf[0] = h0
    tmf[1] = h1
    energy = h0 * h0 + h1 * h1
    rows16 = iota((16, 1), 0)

    def column(l):
        col = jnp.zeros((16, 1), I32)
        for m in range(NT):
            col = jnp.where(rows16 == m, bounds_ref[m, l], col)
        return col

    edges = [jnp.zeros((16, 1), I32)] + [column(l) for l in range(15)] + [jnp.full((16, 1), F, I32)]
    total = jnp.zeros((16, 1), F32)
    powers = jnp.zeros((16, 128), F32)
    for l in range(NBINS):
        inside = (freq >= edges[l]) & (freq < edges[l + 1])
        band = jnp.sum(jnp.where(inside, energy, 0.0), axis=1, keepdims=True) + EPSILON
        total = total + band
        powers = jnp.where(lane == l, band, powers)
    inverse = jnp.broadcast_to(1.0 / total, (16, 128))
    itp[...] = inverse
    for m in range(NT):
        low = jnp.zeros((16, 128), I32)
        high = jnp.full((16, 128), F, I32)
        for l in range(15):
            low = jnp.where(sub == l + 1, bounds_ref[m, l], low)
            high = jnp.where(sub == l, bounds_ref[m, l], high)
        touch = (cls == quarter) & (low < 128 * chunk + 128) & (high > 128 * chunk)
        whole = jnp.where((sub == 0) & (lane < 96), 1.0, 0.0)
        pick[m] = jnp.concatenate([jnp.where(touch, 1.0, 0.0), whole], 0)[:, :96].astype(BF)
        own = jnp.where(sub == lane, jnp.broadcast_to(powers[m : m + 1], (16, 128)), 0.0)
        own = jnp.sum(own, axis=1, keepdims=True)
        first = jnp.broadcast_to(1.0 / own, (16, 128))
        second = jnp.where(sub == 0, -jnp.broadcast_to(inverse[m : m + 1], (16, 128)), 0.0)
        weight[m] = jnp.concatenate([first, second], 0) * (1.0 / (2.0 * (NBINS - 1)))
        index = jnp.zeros((32, 128), I32)
        for l in range(15):
            index = index + jnp.where(nat >= bounds_ref[m, l], 1, 0)
        index = index - 3 * ((index * 11) >> 5)
        for q in range(3):
            masks[m, q] = jnp.where(index == q, 1.0, 0.0).astype(BF)


def spread(g_ref, rot_ref, turned, nat, sre, sim, group):
    rc, rs = rot_ref[0], rot_ref[1]
    for q in range(4):
        for k in range(8):
            a = group * 8 + k
            re = g_ref[a, pl.ds(32 * q, 32), :].astype(F32)
            im = g_ref[a, pl.ds(ROWS_A + 32 * q, 32), :].astype(F32)
            tr = re * rc - im * rs
            ti = re * rs + im * rc
            turned[a, q] = tr.astype(BF)
            turned[a, 4 + q] = ti.astype(BF)
            nat[0, q, pl.ds(k * 32, 32), :] = tr
            nat[1, q, pl.ds(k * 32, 32), :] = ti
    for q in range(4):
        for c in range(32):
            sre[group, pl.ds(8 * q, 8), pl.ds(c * 128, 128)] = nat[0, q, pl.ds(c, 8, stride=32), :]
            sim[group, pl.ds(8 * q, 8), pl.ds(c * 128, 128)] = nat[1, q, pl.ds(c, 8, stride=32), :]


def filters(table_ref, tmf, itp, sre, sim, lhs, snr_ref, peak, group, first):
    for n in range(4):
        for k in range(F // 256):
            cut = pl.ds(k * 256, 256)
            h0 = tmf[0, pl.ds(first + n, 1), cut]
            h1 = tmf[1, pl.ds(first + n, 1), cut]
            re = sre[group, :, cut]
            im = sim[group, :, cut]
            lhs[pl.ds(64 * n, 32), cut] = (re * h0 + im * h1).astype(BF)
            lhs[pl.ds(64 * n + 32, 32), cut] = (im * h0 - re * h1).astype(BF)
    acc = jnp.dot(lhs[...], table_ref[...], preferred_element_type=F32)
    back = 127 - iota((16, 128), 1)
    for n in range(4):
        a = acc[64 * n : 64 * n + 32, :128]
        d = acc[64 * n : 64 * n + 32, 128:]
        c = acc[64 * n + 32 : 64 * n + 64, :128]
        b = acc[64 * n + 32 : 64 * n + 64, 128:]
        plus = (a - b) * (a - b) + (c + d) * (c + d)
        minus = (a + b) * (a + b) + (c - d) * (c - d)
        scale = itp[pl.ds(first + n, 1), :]
        plus = (plus[:16] + plus[16:]) * scale
        minus = (minus[:16] + minus[16:]) * scale
        top = jnp.maximum(plus, minus)
        top = jnp.maximum(top[:8], top[8:])
        peak[first + n] = jnp.maximum(peak[first + n], top)
        minus = jnp.take_along_axis(minus, back, axis=1)
        for r in range(2):
            snr_ref[first + n, pl.ds(group * 32 + r, 8, stride=4), :] = minus[8 * r : 8 * r + 8]
            snr_ref[first + n, pl.ds(group * 32 + 2 + r, 8, stride=4), :] = plus[8 * r : 8 * r + 8]


def veto(w0_ref, far_ref, tn_ref, meta, turned, masks, pick, weight, chi_ref, a):
    fc, fs = far_ref[0], far_ref[1]
    lane = iota((1, 128), 1)
    rows = []
    at = []
    for k in range(4):
        m, r, blk = meta[a, k], meta[a, 4 + k], meta[a, 8 + k]
        at.append((m, blk))
        h0, h1 = tn_ref[0, m], tn_ref[1, m]
        sign = (2 * blk - 1).astype(F32).astype(BF)
        for d in range(2):
            re = turned[a, 2 * d + r]
            im = turned[a, 4 + 2 * d + r]
            xr = re * h0 + im * h1
            xi = (im * h0 - re * h1) * sign
            for q in range(3):
                mask = masks[m, q]
                rows.append(jnp.concatenate([xr * mask, xi * mask], 1))
    part = jnp.dot(jnp.concatenate(rows, 0), w0_ref[...], preferred_element_type=F32).astype(BF)
    for k in range(4):
        m, blk = at[k]
        s = jnp.zeros((32, 128), F32)
        for d in range(2):
            base = (2 * k + d) * 96
            turns = []
            for q in range(3):
                ur = part[base + 32 * q : base + 32 * q + 32, :128]
                ui = part[base + 32 * q : base + 32 * q + 32, 128:]
                turns.append(jnp.concatenate([ur * fc - ui * fs, ur * fs + ui * fc], 1))
            bands = jnp.dot(pick[m], jnp.concatenate(turns, 0), preferred_element_type=F32)
            s = s + bands[:, :128] * bands[:, :128] + bands[:, 128:] * bands[:, 128:]
        line = jnp.sum(s * weight[m], axis=0, keepdims=True)
        index = jnp.where(blk == 1, lane, 127 - lane)
        line = jnp.take_along_axis(
            jnp.broadcast_to(line, (8, 128)), jnp.broadcast_to(index, (8, 128)), axis=1
        )
        chi_ref[a, pl.ds(k, 1), :] = line[0:1]


def requests(g_ref, wanted):
    shard = lax.axis_index("tmpl").astype(F32)
    rows = [g_ref[:, 128 + v, :].astype(F32) for v in range(4)]
    lane = iota((32, 128), 1)
    hit = (rows[0] == shard) & (lane < 64)
    before = jnp.where(iota((128, 128), 0) < iota((128, 128), 1), 1.0, 0.0).astype(BF)
    rank = jnp.dot(jnp.where(hit, 1.0, 0.0).astype(BF), before, preferred_element_type=F32)
    table = jnp.zeros((32, 128), F32)
    for v in range(3):
        for k in range(4):
            value = jnp.sum(jnp.where(hit & (rank == float(k)), rows[v + 1], 0.0), axis=1, keepdims=True)
            table = jnp.where(lane == 4 * v + k, value, table)
    wanted[...] = table.astype(I32)


def compute_kernel(
    g_ref, tm_ref, tn_ref, bounds_ref, table_ref, rot_ref, w0_ref, far_ref,
    snr_ref, peak_ref, chi_ref,
    tmf, itp, masks, pick, weight, turned, nat, sre, sim, lhs, peak, wanted, meta, sem,
):
    requests(g_ref, wanted)
    copy = pltpu.make_async_copy(wanted, meta, sem)
    copy.start()
    prepare(tm_ref, bounds_ref, tmf, itp, masks, pick, weight)
    chi_ref[...] = jnp.zeros_like(chi_ref)
    peak[...] = jnp.zeros_like(peak)
    copy.wait()

    @pl.loop(0, 4)
    def _(group):
        spread(g_ref, rot_ref, turned, nat, sre, sim, group)

    @pl.loop(0, 16)
    def _(step):
        filters(table_ref, tmf, itp, sre, sim, lhs, snr_ref, peak, step // 4, (step % 4) * 4)

    @pl.loop(0, 32)
    def _(a):
        veto(w0_ref, far_ref, tn_ref, meta, turned, masks, pick, weight, chi_ref, a)

    for m in range(NT):
        peak_ref[pl.ds(m, 1), :] = jnp.max(peak[m], axis=0, keepdims=True)


def compute(gathered, templates, bounds, wave, rot, w0, far):
    vmem = pl.BlockSpec(memory_space=pltpu.VMEM)
    smem = pl.BlockSpec(memory_space=pltpu.SMEM)
    return pl.pallas_call(
        compute_kernel,
        out_shape=(
            jax.ShapeDtypeStruct((NT, 128, 128), F32),
            jax.ShapeDtypeStruct((NT, 128), F32),
            jax.ShapeDtypeStruct((32, 8, 128), F32),
        ),
        in_specs=[vmem, vmem, vmem, smem, vmem, vmem, vmem, vmem],
        out_specs=(vmem, vmem, vmem),
        scratch_shapes=[
            pltpu.VMEM((2, NT, F), F32),
            pltpu.VMEM((NT, 128), F32),
            pltpu.VMEM((NT, 3, 32, 128), BF),
            pltpu.VMEM((NT, 32, 96), BF),
            pltpu.VMEM((NT, 32, 128), F32),
            pltpu.VMEM((32, 8, 32, 128), BF),
            pltpu.VMEM((2, 4, 256, 128), F32),
            pltpu.VMEM((4, 32, F), F32),
            pltpu.VMEM((4, 32, F), F32),
            pltpu.VMEM((256, F), BF),
            pltpu.VMEM((NT, 8, 128), F32),
            pltpu.VMEM((32, 128), I32),
            pltpu.SMEM((32, 128), I32),
            pltpu.SemaphoreType.DMA,
        ],
        compiler_params=pltpu.CompilerParams(vmem_limit_bytes=48 * 1024 * 1024),
        name="compute",
    )(gathered, templates, templates.reshape(2, NT, 32, 128), bounds, wave, rot, w0, far)


def home_kernel(chi_ref, peak_ref, owner_ref, out_ref, loud_ref, slots, peaks, send_sem, recv_sem, pair_send, pair_recv):
    me = lax.axis_index("tmpl")
    seg = lax.axis_index("seg")
    barrier = pltpu.get_barrier_semaphore()
    for j in range(1, 32):
        pl.semaphore_signal(barrier, inc=1, device_id=((me + j) % 32, seg), device_id_type=MESH)
    for j in range(1, 4):
        pl.semaphore_signal(barrier, inc=1, device_id=(me, (seg + j) % 4), device_id_type=MESH)
    pl.semaphore_wait(barrier, 34)
    copies = []
    for j in range(1, 32):
        peer = (me + j) % 32
        copies.append(
            pltpu.make_async_remote_copy(
                src_ref=chi_ref.at[peer],
                dst_ref=slots.at[me],
                send_sem=send_sem.at[j],
                recv_sem=recv_sem.at[j],
                device_id=(peer, seg),
                device_id_type=MESH,
            )
        )
    for j in range(1, 4):
        copies.append(
            pltpu.make_async_remote_copy(
                src_ref=peak_ref,
                dst_ref=peaks.at[j],
                send_sem=pair_send.at[j],
                recv_sem=pair_recv.at[j],
                device_id=(me, (seg + j) % 4),
                device_id_type=MESH,
            )
        )
    for copy in copies:
        copy.start()
    slots[pl.ds(me, 1)] = chi_ref[pl.ds(me, 1)]
    owner = owner_ref[...]
    i, j = iota((64, 64), 0), iota((64, 64), 1)
    across = jnp.sum(jnp.where(i == j, owner, 0), axis=0, keepdims=True)
    rank = jnp.sum(jnp.where((j < i) & (across == owner), 1, 0), axis=1, keepdims=True)
    choose = jnp.where(iota((64, 256), 1) == owner * 8 + rank, 1.0, 0.0)
    for copy in copies:
        copy.wait()
    out_ref[...] = jnp.dot(
        choose,
        slots[...].reshape(256, 128),
        preferred_element_type=F32,
        precision=lax.Precision.HIGHEST,
    )
    top = jnp.maximum(jnp.maximum(peak_ref[...], peaks[1]), jnp.maximum(peaks[2], peaks[3]))
    top = jnp.max(top, axis=1, keepdims=True)
    loud_ref[...] = jnp.max(jnp.where(iota((NT, 128), 0) == iota((NT, 128), 1), top, 0.0), axis=0, keepdims=True)


def home(chi, peak, owner):
    vmem = pl.BlockSpec(memory_space=pltpu.VMEM)
    return pl.pallas_call(
        home_kernel,
        out_shape=(jax.ShapeDtypeStruct((64, 128), F32), jax.ShapeDtypeStruct((1, 128), F32)),
        in_specs=[vmem] * 3,
        out_specs=(vmem, vmem),
        scratch_shapes=[
            pltpu.VMEM((32, 8, 128), F32),
            pltpu.VMEM((4, NT, 128), F32),
            pltpu.SemaphoreType.DMA((32,)),
            pltpu.SemaphoreType.DMA((32,)),
            pltpu.SemaphoreType.DMA((4,)),
            pltpu.SemaphoreType.DMA((4,)),
        ],
        compiler_params=pltpu.CompilerParams(collective_id=1, has_side_effects=True),
        name="home",
    )(chi, peak, owner)


def body(
    spectra, templates, bounds, trigger_owner, trigger_template, trigger_segment, trigger_block
):
    wave, rot, w0, far = tables()
    parts = spectra.reshape(2, 128, 128)
    listed = jnp.stack([trigger_owner[:, 0], trigger_template, trigger_segment, trigger_block])
    listed = jnp.pad(listed.astype(BF), ((0, 12), (0, 64)))
    block = jnp.concatenate([parts[0], listed, parts[1]], axis=0)
    gathered = gather(block)
    snr, peak, chi = compute(gathered, templates, bounds, wave, rot, w0, far)
    chisq, loud = home(chi, peak, trigger_owner)
    snr = snr.reshape(NT, 32, 2, 2, 128).transpose(0, 1, 3, 2, 4).reshape(NT, 32, 2, 256)
    return snr, loud[0, :NT], chisq


def solution(mesh):
    in_specs = (
        P(None, None, "tmpl", "seg", None),
        P(None, "tmpl", None),
        P("tmpl", None),
        P(("tmpl", "seg"), None),
        P(("tmpl", "seg")),
        P(("tmpl", "seg")),
        P(("tmpl", "seg")),
    )
    out_specs = (P("tmpl", None, "seg", None), P("tmpl"), P(("tmpl", "seg"), None))
    return jax.shard_map(body, mesh=mesh, in_specs=in_specs, out_specs=out_specs, check_vma=False)
```

```python
import math

import jax
import jax.numpy as jnp
import numpy as np
from jax import lax
from jax.experimental import pallas as pl
from jax.experimental.pallas import tpu as pltpu
from jax.sharding import PartitionSpec as P

F = 4096
NT = 16
NBINS = 16
EPSILON = 1e-06
BF = jnp.bfloat16
F32 = jnp.float32
I32 = jnp.int32
MESH = pl.DeviceIdType.MESH
ROWS_A = 144
ROWS = 272


def tables():
    step = 2.0 * math.pi / 4096.0
    phi = np.arange(4096, dtype=np.float64) - 2048.0
    half = np.arange(128, dtype=np.float64) + 0.5
    ang = step * phi[:, None] * half[None, :]
    main = np.concatenate([np.cos(ang), np.sin(ang)], 1)
    turn = (step * 127.5 * phi).reshape(32, 128)
    rot = np.stack([np.cos(turn), np.sin(turn)])
    near = step * np.arange(128.0)[:, None] * half[None, :]
    w0 = np.concatenate(
        [
            np.concatenate([np.cos(near), np.sin(near)], 1),
            np.concatenate([-np.sin(near), np.cos(near)], 1),
        ],
        0,
    )
    far = step * (128.0 * np.arange(32.0) - 2048.0)[:, None] * half[None, :]
    far = np.stack([np.cos(far), np.sin(far)])
    return (
        jnp.asarray(main, F32).astype(BF),
        jnp.asarray(rot, F32),
        jnp.asarray(w0, F32).astype(BF),
        jnp.asarray(far, F32).astype(BF),
    )


def iota(shape, dim):
    return lax.broadcasted_iota(I32, shape, dim)


def ring(zz, xx, yy):
    return zz * 16 + xx % 4 * 4 + yy % 4


class Torus:
    def __init__(self, held, full_sem, half_sem, recv_sem):
        self.me = lax.axis_index("tmpl")
        self.seg = lax.axis_index("seg")
        self.z, self.x, self.y = self.me // 16, self.me // 4 % 4, self.me % 4
        self.held, self.full_sem, self.half_sem, self.recv_sem = held, full_sem, half_sem, recv_sem

    def step(self, kind, near, far, here=False):
        plane = self.z if kind == 0 else 1 - self.z
        xx = self.x + near * (1 - plane) + far * plane
        yy = self.y + near * plane + far * (1 - plane)
        return ring(self.z if here else plane, xx, yy)

    def member(self, delta, k):
        plane, at = k // 4, k % 4
        first = at * 4 + (self.y + delta) % 4
        second = 16 + (self.x + delta) % 4 * 4 + at
        return (1 - plane) * first + plane * second

    def copy(self, source, peer, half, sem):
        if half is None:
            view, recv, send = self.held.at[source], self.recv_sem.at[0, source], self.full_sem.at[sem]
        else:
            cut = pl.ds(0, ROWS_A) if half == 0 else pl.ds(ROWS_A, ROWS - ROWS_A)
            view, recv, send = self.held.at[source, cut], self.recv_sem.at[half, source], self.half_sem.at[half, sem]
        return pltpu.make_async_remote_copy(
            src_ref=view, dst_ref=view, send_sem=send, recv_sem=recv, device_id=(peer, self.seg), device_id_type=MESH
        )

    def arrive(self, source, halves=False):
        peer = ring(1 - self.z, self.x, self.y)
        for half in (0, 1) if halves else (None,):
            self.copy(source, peer, half, 0).wait_recv()

    def fan(self, kind, near):
        source = self.step(kind, near, 0)
        for n, far in enumerate((1, 3)):
            self.copy(source, self.step(kind, 0, far, True), None, 5 + kind * 8 + near * 2 + n).start()

    def sides(self, kind):
        source = self.step(kind, 0, 0)
        for n, near in enumerate((1, 3)):
            self.copy(source, self.step(kind, near, 0, True), None, 1 + kind * 2 + n).start()

    def begin(self):
        mate = ring(1 - self.z, self.x, self.y)
        self.copy(self.me, mate, None, 0).start()
        self.sides(0)
        self.fan(0, 0)

    def first(self):
        self.arrive(self.step(1, 0, 0))
        self.sides(1)
        self.fan(1, 0)
        for near in (1, 3):
            for kind in (0, 1):
                source = self.step(kind, near, 0)
                self.arrive(source)
                self.copy(source, self.step(kind, 4 - near, 0, True), 1 if near == 1 else 0, kind).start()
                self.fan(kind, near)
        for kind in (0, 1):
            self.arrive(self.step(kind, 2, 0), True)
            self.fan(kind, 2)

    def onward(self, near):
        for kind in (0, 1):
            for far in (1, 3):
                source = self.step(kind, near, far)
                self.arrive(source)
                self.copy(source, self.step(kind, 0, 4 - far, True), 1 if far == 1 else 0, 2 + kind * 4 + near).start()

    def last(self):
        @pl.loop(0, 4)
        def _(near):
            for kind in (0, 1):
                self.arrive(self.step(kind, near, 2), True)

    def finish(self):
        peer = ring(1 - self.z, self.x, self.y)

        @pl.loop(0, 21)
        def _(n):
            self.copy(self.me, peer, None, n).wait_send()

        @pl.loop(0, 10)
        def _(n):
            for half in (0, 1):
                self.copy(self.me, peer, half, n).wait_send()


def lay_out(spec_ref, own_ref, tmpl_ref, seg_ref, blk_ref, tm_ref, held, tn, nat, listed, me):
    listed[...] = jnp.zeros_like(listed)
    for v, ref in enumerate((own_ref, tmpl_ref, seg_ref, blk_ref)):
        listed[pl.ds(v, 1), pl.ds(0, 64)] = ref[...].astype(F32)
    held[me, pl.ds(128, 16), :] = listed[...].astype(BF)
    for p in range(2):
        for d in range(2):
            value = spec_ref[p, d].astype(F32)
            for c in range(32):
                nat[p, d, pl.ds(c, 2, stride=32), :] = value[:, 128 * c : 128 * c + 128]
    for p in range(2):
        for d in range(2):
            held[me, pl.ds(p * ROWS_A + 64 * d, 64), :] = nat[p, d, pl.ds(0, 64), :].astype(BF)


def prepare(tm_ref, bounds_ref, tmf, tn, nat, itp, masks, pick, weight):
    lane = iota((16, 128), 1)
    sub = iota((16, 128), 0)
    quarter, chunk = lane // 32, lane % 32
    cls = sub % 3
    natural = iota((32, 128), 0) * 128 + iota((32, 128), 1)
    freq = iota((16, F), 1)
    h0 = tm_ref[0].astype(F32)
    h1 = tm_ref[1].astype(F32)
    tmf[0] = h0
    tmf[1] = h1
    for p in range(2):
        for h in range(2):
            for c in range(32):
                nat[p, h, pl.ds(c, 8, stride=32), :] = tmf[p, pl.ds(8 * h, 8), pl.ds(128 * c, 128)]
            for m in range(8):
                tn[p, 8 * h + m] = nat[p, h, pl.ds(32 * m, 32), :].astype(BF)
    energy = h0 * h0 + h1 * h1
    rows16 = iota((16, 1), 0)

    def column(l):
        col = jnp.zeros((16, 1), I32)
        for m in range(NT):
            col = jnp.where(rows16 == m, bounds_ref[m, l], col)
        return col

    edges = [jnp.zeros((16, 1), I32)] + [column(l) for l in range(15)] + [jnp.full((16, 1), F, I32)]
    total = jnp.zeros((16, 1), F32)
    powers = jnp.zeros((16, 128), F32)
    for l in range(NBINS):
        inside = (freq >= edges[l]) & (freq < edges[l + 1])
        band = jnp.sum(jnp.where(inside, energy, 0.0), axis=1, keepdims=True) + EPSILON
        total = total + band
        powers = jnp.where(lane == l, band, powers)
    inverse = jnp.broadcast_to(1.0 / total, (16, 128))
    itp[...] = inverse
    none = jnp.zeros((16, 96), F32)
    short = iota((16, 96), 0)
    sums = jnp.concatenate([jnp.where(short == 0, 1.0, none), jnp.where(short == 1, 1.0, none)], 1)
    for m in range(NT):
        low = jnp.zeros((16, 128), I32)
        high = jnp.full((16, 128), F, I32)
        index = jnp.zeros((32, 128), I32)
        for l in range(15):
            edge = bounds_ref[m, l]
            low = jnp.where(sub == l + 1, edge, low)
            high = jnp.where(sub == l, edge, high)
            index = index + jnp.where(natural >= edge, 1, 0)
        touch = (cls == quarter) & (low < 128 * chunk + 128) & (high > 128 * chunk)
        touch = jnp.where(touch, 1.0, 0.0)[:, :96]
        pick[m] = jnp.concatenate(
            [jnp.concatenate([touch, none], 1), jnp.concatenate([none, touch], 1), sums], 0
        ).astype(BF)
        own = jnp.where(sub == lane, jnp.broadcast_to(powers[m : m + 1], (16, 128)), 0.0)
        own = jnp.sum(own, axis=1, keepdims=True)
        bands = jnp.broadcast_to(1.0 / own, (16, 128))
        whole = jnp.where(sub < 2, -jnp.broadcast_to(inverse[m : m + 1], (16, 128)), 0.0)
        weight[m] = jnp.concatenate([bands, bands, whole], 0) * (1.0 / (2.0 * (NBINS - 1)))
        index = index - 3 * ((index * 11) >> 5)
        for q in range(3):
            masks[m, q] = jnp.where(index == q, 1.0, 0.0).astype(BF)


def spread(place, held, rot_ref, turned, nat, sre, sim, delta):
    rc, rs = rot_ref[0], rot_ref[1]

    @pl.loop(0, 8)
    def _(k):
        a = place.member(delta, k)
        for q in range(4):
            re = held[a, pl.ds(32 * q, 32), :].astype(F32)
            im = held[a, pl.ds(ROWS_A + 32 * q, 32), :].astype(F32)
            tr = re * rc - im * rs
            ti = re * rs + im * rc
            turned[k, q] = tr.astype(BF)
            turned[k, 4 + q] = ti.astype(BF)
            nat[0, q, pl.ds(k * 32, 32), :] = tr
            nat[1, q, pl.ds(k * 32, 32), :] = ti

    for q in range(4):
        for c in range(32):
            sre[pl.ds(8 * q, 8), pl.ds(c * 128, 128)] = nat[0, q, pl.ds(c, 8, stride=32), :]
            sim[pl.ds(8 * q, 8), pl.ds(c * 128, 128)] = nat[1, q, pl.ds(c, 8, stride=32), :]


def requests(place, held, wanted, meta, sem, delta):
    shard = place.me.astype(F32)
    tiles = [held[place.member(delta, k), pl.ds(128, 16), :].astype(F32) for k in range(8)]
    rows = [jnp.concatenate([t[v : v + 1] for t in tiles], 0) for v in range(4)]
    lane = iota((8, 128), 1)
    hit = (rows[0] == shard) & (lane < 64)
    before = jnp.where(iota((128, 128), 0) < iota((128, 128), 1), 1.0, 0.0).astype(BF)
    rank = jnp.dot(jnp.where(hit, 1.0, 0.0).astype(BF), before, preferred_element_type=F32)
    table = jnp.zeros((8, 128), F32)
    for v in range(3):
        for k in range(4):
            value = jnp.sum(jnp.where(hit & (rank == float(k)), rows[v + 1], 0.0), axis=1, keepdims=True)
            table = jnp.where(lane == 4 * v + k, value, table)
    wanted[...] = table.astype(I32)
    copy = pltpu.make_async_copy(wanted, meta, sem)
    copy.start()
    copy.wait()


def veto(w0_ref, far_ref, tn, meta, turned, masks, pick, weight, chi, slot, source):
    fc, fs = far_ref[0], far_ref[1]
    rows = []
    at = []
    for k in range(4):
        m = jnp.clip(meta[slot, k], 0, NT - 1)
        r = jnp.clip(meta[slot, 4 + k], 0, 1)
        blk = jnp.clip(meta[slot, 8 + k], 0, 1)
        at.append((m, blk))
        h0, h1 = tn[0, m], tn[1, m]
        sign = (2 * blk - 1).astype(F32).astype(BF)
        for d in range(2):
            re = turned[slot, 2 * d + r]
            im = turned[slot, 4 + 2 * d + r]
            xr = re * h0 + im * h1
            xi = (im * h0 - re * h1) * sign
            for q in range(3):
                mask = masks[m, q]
                rows.append(jnp.concatenate([xr * mask, xi * mask], 1))
    part = jnp.dot(jnp.concatenate(rows, 0), w0_ref[...], preferred_element_type=F32).astype(BF)
    lines = []
    for k in range(4):
        m, blk = at[k]
        turns = []
        for q in range(6):
            base = k * 192 + 32 * q
            ur = part[base : base + 32, :128]
            ui = part[base : base + 32, 128:]
            turns.append(jnp.concatenate([ur * fc - ui * fs, ur * fs + ui * fc], 1))
        bands = jnp.dot(pick[m], jnp.concatenate(turns, 0), preferred_element_type=F32)
        s = bands[:, :128] * bands[:, :128] + bands[:, 128:] * bands[:, 128:]
        lines.append((blk, jnp.sum(s * weight[m], axis=0, keepdims=True)))
    value = jnp.concatenate([line for _, line in lines] * 2, 0)
    back = jnp.take_along_axis(value, 127 - iota((8, 128), 1), axis=1)
    sub = iota((8, 128), 0) % 4
    late = jnp.zeros((8, 128), I32)
    for k in range(4):
        late = jnp.where(sub == k, lines[k][0], late)
    chi[source] = jnp.where(late == 1, value, back)


def filters(place, table_ref, tmf, itp, sre, sim, lhs, snr_ref, peak, delta, first):
    for n in range(4):
        for k in range(F // 256):
            cut = pl.ds(k * 256, 256)
            h0 = tmf[0, pl.ds(first + n, 1), cut]
            h1 = tmf[1, pl.ds(first + n, 1), cut]
            re = sre[:, cut]
            im = sim[:, cut]
            lhs[pl.ds(64 * n, 32), cut] = (re * h0 + im * h1).astype(BF)
            lhs[pl.ds(64 * n + 32, 32), cut] = (im * h0 - re * h1).astype(BF)
    acc = jnp.dot(lhs[...], table_ref[...], preferred_element_type=F32)
    back = 127 - iota((16, 128), 1)
    one = (place.y + delta) % 4 * 4
    two = 64 + (place.x + delta) % 4 * 16
    for n in range(4):
        a = acc[64 * n : 64 * n + 32, :128]
        d = acc[64 * n : 64 * n + 32, 128:]
        c = acc[64 * n + 32 : 64 * n + 64, :128]
        b = acc[64 * n + 32 : 64 * n + 64, 128:]
        plus = (a - b) * (a - b) + (c + d) * (c + d)
        minus = (a + b) * (a + b) + (c - d) * (c - d)
        scale = itp[pl.ds(first + n, 1), :]
        plus = (plus[:16] + plus[16:]) * scale
        minus = (minus[:16] + minus[16:]) * scale
        top = jnp.maximum(plus, minus)
        top = jnp.maximum(top[:8], top[8:])
        peak[first + n] = jnp.maximum(peak[first + n], top)
        minus = jnp.take_along_axis(minus, back, axis=1)
        for half, value in enumerate((minus, plus)):
            for r in range(2):
                to = 2 * half + r
                snr_ref[first + n, pl.ds(one + to, 4, stride=16), :] = value[8 * r : 8 * r + 4]
                for k in range(4):
                    line = value[8 * r + 4 + k : 8 * r + 5 + k]
                    snr_ref[first + n, pl.ds(two + to + 4 * k, 1), :] = line


def kernel(
    spec_ref, tm_ref, bounds_ref, own_ref, tmpl_ref, seg_ref, blk_ref, table_ref, rot_ref, w0_ref, far_ref,
    snr_ref, loud_ref, out_ref,
    held, listed, tmf, tn, itp, masks, pick, weight, turned, nat, sre, sim, lhs, peak, wanted, meta,
    chi, slots, tops, peaks,
    full_sem, half_sem, recv_sem, meta_sem, chi_send, chi_recv, pair_send, pair_recv,
):
    place = Torus(held, full_sem, half_sem, recv_sem)
    me, seg = place.me, place.seg
    barrier = pltpu.get_barrier_semaphore()

    @pl.loop(1, 32)
    def _(j):
        pl.semaphore_signal(barrier, inc=1, device_id=((me + j) % 32, seg), device_id_type=MESH)

    for j in range(1, 4):
        pl.semaphore_signal(barrier, inc=1, device_id=(me, (seg + j) % 4), device_id_type=MESH)
    lay_out(spec_ref, own_ref, tmpl_ref, seg_ref, blk_ref, tm_ref, held, tn, nat, listed, me)
    pl.semaphore_wait(barrier, 34)
    place.begin()
    prepare(tm_ref, bounds_ref, tmf, tn, nat, itp, masks, pick, weight)
    peak[...] = jnp.zeros_like(peak)
    place.first()

    def result(source):
        return pltpu.make_async_remote_copy(
            src_ref=chi.at[source],
            dst_ref=slots.at[me],
            send_sem=chi_send.at[source],
            recv_sem=chi_recv.at[me],
            device_id=(source, seg),
            device_id_type=MESH,
        )

    def group(delta, between):
        spread(place, held, rot_ref, turned, nat, sre, sim, delta)
        requests(place, held, wanted, meta, meta_sem, delta)

        @pl.loop(0, 2)
        def _(part):
            for n in range(4):
                slot = part * 4 + n
                source = place.member(delta, slot)
                veto(w0_ref, far_ref, tn, meta, turned, masks, pick, weight, chi, slot, source)

        @pl.loop(0, 8)
        def _(k):
            source = place.member(delta, k)

            @pl.when(source != me)
            def _():
                result(source).start()

        @pl.loop(0, 4)
        def _(step):
            filters(place, table_ref, tmf, itp, sre, sim, lhs, snr_ref, peak, delta, step * 4)
            if between is not None:
                between(step)

    group(0, lambda step: place.onward(step + step // 2 * (1 - 2 * (step % 2))))

    @pl.loop(0, 2)
    def _(n):
        group(1 + 2 * n, None)

    place.last()
    group(2, None)

    slots[pl.ds(me, 1)] = chi[pl.ds(me, 1)]
    tops[...] = jnp.concatenate([jnp.max(peak[m], axis=0, keepdims=True) for m in range(NT)], 0)
    pairs = [
        pltpu.make_async_remote_copy(
            src_ref=tops,
            dst_ref=peaks.at[j],
            send_sem=pair_send.at[j],
            recv_sem=pair_recv.at[j],
            device_id=(me, (seg + j) % 4),
            device_id_type=MESH,
        )
        for j in range(1, 4)
    ]
    for copy in pairs:
        copy.start()

    @pl.loop(0, 32)
    def _(other):
        @pl.when(other != me)
        def _():
            pltpu.make_async_remote_copy(
                src_ref=chi.at[other],
                dst_ref=slots.at[other],
                send_sem=chi_send.at[other],
                recv_sem=chi_recv.at[other],
                device_id=(other, seg),
                device_id_type=MESH,
            ).wait()

    i, j = iota((64, 64), 0), iota((64, 64), 1)
    across = own_ref[...]
    owner = jnp.sum(jnp.where(i == j, across, 0), axis=1, keepdims=True)
    rank = jnp.sum(jnp.where((j < i) & (across == owner), 1, 0), axis=1, keepdims=True)
    choose = jnp.where(iota((64, 256), 1) == owner * 8 + rank, 1.0, 0.0)
    out_ref[...] = jnp.dot(
        choose, slots[...].reshape(256, 128), preferred_element_type=F32, precision=lax.Precision.HIGHEST
    )
    place.finish()
    for copy in pairs:
        copy.wait()
    top = jnp.maximum(jnp.maximum(tops[...], peaks[1]), jnp.maximum(peaks[2], peaks[3]))
    top = jnp.max(top, axis=1, keepdims=True)
    loud = jnp.max(jnp.where(iota((NT, 128), 0) == iota((NT, 128), 1), top, 0.0), axis=0, keepdims=True)
    loud_ref[...] = loud[:, :NT]


def body(
    spectra, templates, bounds, trigger_owner, trigger_template, trigger_segment, trigger_block
):
    vmem = pl.BlockSpec(memory_space=pltpu.VMEM)
    smem = pl.BlockSpec(memory_space=pltpu.SMEM)
    dma = pltpu.SemaphoreType.DMA
    snr, loud, chisq = pl.pallas_call(
        kernel,
        out_shape=(
            jax.ShapeDtypeStruct((NT, 128, 128), F32),
            jax.ShapeDtypeStruct((1, NT), F32),
            jax.ShapeDtypeStruct((64, 128), F32),
        ),
        in_specs=[vmem, vmem, smem] + [vmem] * 8,
        out_specs=(vmem, vmem, vmem),
        scratch_shapes=[
            pltpu.VMEM((32, ROWS, 128), BF),
            pltpu.VMEM((16, 128), F32),
            pltpu.VMEM((2, NT, F), F32),
            pltpu.VMEM((2, NT, 32, 128), BF),
            pltpu.VMEM((NT, 128), F32),
            pltpu.VMEM((NT, 3, 32, 128), BF),
            pltpu.VMEM((NT, 48, 192), BF),
            pltpu.VMEM((NT, 48, 128), F32),
            pltpu.VMEM((8, 8, 32, 128), BF),
            pltpu.VMEM((2, 4, 288, 128), F32),
            pltpu.VMEM((32, F), F32),
            pltpu.VMEM((32, F), F32),
            pltpu.VMEM((256, F), BF),
            pltpu.VMEM((NT, 8, 128), F32),
            pltpu.VMEM((8, 128), I32),
            pltpu.SMEM((8, 128), I32),
            pltpu.VMEM((32, 8, 128), F32),
            pltpu.VMEM((32, 8, 128), F32),
            pltpu.VMEM((NT, 128), F32),
            pltpu.VMEM((4, NT, 128), F32),
            dma((21,)),
            dma((2, 10)),
            dma((2, 32)),
            dma,
            dma((32,)),
            dma((32,)),
            dma((4,)),
            dma((4,)),
        ],
        compiler_params=pltpu.CompilerParams(
            collective_id=0, has_side_effects=True, vmem_limit_bytes=48 * 1024 * 1024
        ),
        name="search",
    )(
        spectra.reshape(2, 2, 2, F),
        templates,
        bounds,
        trigger_owner.reshape(1, 64),
        trigger_template.reshape(1, 64),
        trigger_segment.reshape(1, 64),
        trigger_block.reshape(1, 64),
        *tables(),
    )
    snr = snr.reshape(NT, 32, 2, 2, 128).transpose(0, 1, 3, 2, 4).reshape(NT, 32, 2, 256)
    return snr, loud.reshape(NT), chisq


def solution(mesh):
    in_specs = (
        P(None, None, "tmpl", "seg", None),
        P(None, "tmpl", None),
        P("tmpl", None),
        P(("tmpl", "seg"), None),
        P(("tmpl", "seg")),
        P(("tmpl", "seg")),
        P(("tmpl", "seg")),
    )
    out_specs = (P("tmpl", None, "seg", None), P("tmpl"), P(("tmpl", "seg"), None))
    return jax.shard_map(body, mesh=mesh, in_specs=in_specs, out_specs=out_specs, check_vma=False)
```

```python
import math

import jax
import jax.numpy as jnp
import numpy as np
from jax import lax
from jax.experimental import pallas as pl
from jax.experimental.pallas import tpu as pltpu
from jax.sharding import PartitionSpec as P

F = 4096
NT = 16
NBINS = 16
EPSILON = 1e-06
BF = jnp.bfloat16
F32 = jnp.float32
I32 = jnp.int32
MESH = pl.DeviceIdType.MESH
ROWS_A = 144
ROWS = 272


def tables():
    step = 2.0 * math.pi / 4096.0
    phi = np.arange(4096, dtype=np.float64) - 2048.0
    half = np.arange(128, dtype=np.float64) + 0.5
    ang = step * phi[:, None] * half[None, :]
    main = np.concatenate([np.cos(ang), np.sin(ang)], 1)
    turn = (step * 127.5 * phi).reshape(32, 128)
    rot = np.stack([np.cos(turn), np.sin(turn)])
    near = step * np.arange(128.0)[:, None] * half[None, :]
    w0 = np.concatenate(
        [
            np.concatenate([np.cos(near), np.sin(near)], 1),
            np.concatenate([-np.sin(near), np.cos(near)], 1),
        ],
        0,
    )
    far = step * (128.0 * np.arange(32.0) - 2048.0)[:, None] * half[None, :]
    far = np.stack([np.cos(far), np.sin(far)])
    return (
        jnp.asarray(main, F32).astype(BF),
        jnp.asarray(rot, F32),
        jnp.asarray(w0, F32).astype(BF),
        jnp.asarray(far, F32).astype(BF),
    )


def iota(shape, dim):
    return lax.broadcasted_iota(I32, shape, dim)


def ring(zz, xx, yy):
    return zz * 16 + xx % 4 * 4 + yy % 4


class Torus:
    def __init__(self, held, full_sem, half_sem, recv_sem):
        self.me = lax.axis_index("tmpl")
        self.seg = lax.axis_index("seg")
        self.z, self.x, self.y = self.me // 16, self.me // 4 % 4, self.me % 4
        self.held, self.full_sem, self.half_sem, self.recv_sem = held, full_sem, half_sem, recv_sem

    def step(self, kind, near, far, here=False):
        plane = self.z if kind == 0 else 1 - self.z
        xx = self.x + near * (1 - plane) + far * plane
        yy = self.y + near * plane + far * (1 - plane)
        return ring(self.z if here else plane, xx, yy)

    def member(self, delta, k):
        plane, at = k // 4, k % 4
        first = at * 4 + (self.y + delta) % 4
        second = 16 + (self.x + delta) % 4 * 4 + at
        return (1 - plane) * first + plane * second

    def copy(self, source, peer, half, sem):
        if half is None:
            view, recv, send = self.held.at[source], self.recv_sem.at[0, source], self.full_sem.at[sem]
        else:
            cut = pl.ds(0, ROWS_A) if half == 0 else pl.ds(ROWS_A, ROWS - ROWS_A)
            view, recv, send = self.held.at[source, cut], self.recv_sem.at[half, source], self.half_sem.at[half, sem]
        return pltpu.make_async_remote_copy(
            src_ref=view, dst_ref=view, send_sem=send, recv_sem=recv, device_id=(peer, self.seg), device_id_type=MESH
        )

    def arrive(self, source, halves=False):
        peer = ring(1 - self.z, self.x, self.y)
        for half in (0, 1) if halves else (None,):
            self.copy(source, peer, half, 0).wait_recv()

    def fan(self, kind, near):
        source = self.step(kind, near, 0)
        for n, far in enumerate((1, 3)):
            self.copy(source, self.step(kind, 0, far, True), None, 5 + kind * 8 + near * 2 + n).start()

    def sides(self, kind):
        source = self.step(kind, 0, 0)
        for n, near in enumerate((1, 3)):
            self.copy(source, self.step(kind, near, 0, True), None, 1 + kind * 2 + n).start()

    def begin(self):
        mate = ring(1 - self.z, self.x, self.y)
        self.copy(self.me, mate, None, 0).start()
        self.sides(0)
        self.fan(0, 0)

    def first(self):
        self.arrive(self.step(1, 0, 0))
        self.sides(1)
        for kind in (0, 1):
            for near in (1, 3):
                source = self.step(kind, near, 0)
                self.arrive(source)
                self.copy(source, self.step(kind, 4 - near, 0, True), 1 if near == 1 else 0, kind).start()
            if kind == 0:
                self.fan(1, 0)
        for kind in (0, 1):
            for near in (1, 3):
                self.fan(kind, near)
        for kind in (0, 1):
            self.arrive(self.step(kind, 2, 0), True)
            self.fan(kind, 2)

    def onward(self, near):
        for kind in (0, 1):
            for far in (1, 3):
                source = self.step(kind, near, far)
                self.arrive(source)
                self.copy(source, self.step(kind, 0, 4 - far, True), 1 if far == 1 else 0, 2 + kind * 4 + near).start()

    def last(self):
        @pl.loop(0, 4)
        def _(near):
            for kind in (0, 1):
                self.arrive(self.step(kind, near, 2), True)

    def finish(self):
        peer = ring(1 - self.z, self.x, self.y)

        @pl.loop(0, 21)
        def _(n):
            self.copy(self.me, peer, None, n).wait_send()

        @pl.loop(0, 10)
        def _(n):
            for half in (0, 1):
                self.copy(self.me, peer, half, n).wait_send()


def lay_out(spec_ref, own_ref, tmpl_ref, seg_ref, blk_ref, tm_ref, held, tn, nat, listed, me):
    listed[...] = jnp.zeros_like(listed)
    for v, ref in enumerate((own_ref, tmpl_ref, seg_ref, blk_ref)):
        listed[pl.ds(v, 1), pl.ds(0, 64)] = ref[...].astype(F32)
    held[me, pl.ds(128, 16), :] = listed[...].astype(BF)
    for p in range(2):
        for d in range(2):
            value = spec_ref[p, d].astype(F32)
            for c in range(32):
                nat[p, d, pl.ds(c, 2, stride=32), :] = value[:, 128 * c : 128 * c + 128]
    for p in range(2):
        for d in range(2):
            held[me, pl.ds(p * ROWS_A + 64 * d, 64), :] = nat[p, d, pl.ds(0, 64), :].astype(BF)


def prepare(tm_ref, bounds_ref, tmf, tn, nat, itp, masks, pick, weight):
    lane = iota((16, 128), 1)
    sub = iota((16, 128), 0)
    quarter, chunk = lane // 32, lane % 32
    cls = sub % 3
    natural = iota((32, 128), 0) * 128 + iota((32, 128), 1)
    freq = iota((16, F), 1)
    h0 = tm_ref[0].astype(F32)
    h1 = tm_ref[1].astype(F32)
    tmf[0] = h0
    tmf[1] = h1
    for p in range(2):
        for h in range(2):
            for c in range(32):
                nat[p, h, pl.ds(c, 8, stride=32), :] = tmf[p, pl.ds(8 * h, 8), pl.ds(128 * c, 128)]
            for m in range(8):
                tn[p, 8 * h + m] = nat[p, h, pl.ds(32 * m, 32), :].astype(BF)
    energy = h0 * h0 + h1 * h1
    rows16 = iota((16, 1), 0)

    def column(l):
        col = jnp.zeros((16, 1), I32)
        for m in range(NT):
            col = jnp.where(rows16 == m, bounds_ref[m, l], col)
        return col

    edges = [jnp.zeros((16, 1), I32)] + [column(l) for l in range(15)] + [jnp.full((16, 1), F, I32)]
    total = jnp.zeros((16, 1), F32)
    powers = jnp.zeros((16, 128), F32)
    for l in range(NBINS):
        inside = (freq >= edges[l]) & (freq < edges[l + 1])
        band = jnp.sum(jnp.where(inside, energy, 0.0), axis=1, keepdims=True) + EPSILON
        total = total + band
        powers = jnp.where(lane == l, band, powers)
    inverse = jnp.broadcast_to(1.0 / total, (16, 128))
    itp[...] = inverse
    none = jnp.zeros((16, 96), F32)
    short = iota((16, 96), 0)
    sums = jnp.concatenate([jnp.where(short == 0, 1.0, none), jnp.where(short == 1, 1.0, none)], 1)
    for m in range(NT):
        low = jnp.zeros((16, 128), I32)
        high = jnp.full((16, 128), F, I32)
        index = jnp.zeros((32, 128), I32)
        for l in range(15):
            edge = bounds_ref[m, l]
            low = jnp.where(sub == l + 1, edge, low)
            high = jnp.where(sub == l, edge, high)
            index = index + jnp.where(natural >= edge, 1, 0)
        touch = (cls == quarter) & (low < 128 * chunk + 128) & (high > 128 * chunk)
        touch = jnp.where(touch, 1.0, 0.0)[:, :96]
        pick[m] = jnp.concatenate(
            [jnp.concatenate([touch, none], 1), jnp.concatenate([none, touch], 1), sums], 0
        ).astype(BF)
        own = jnp.where(sub == lane, jnp.broadcast_to(powers[m : m + 1], (16, 128)), 0.0)
        own = jnp.sum(own, axis=1, keepdims=True)
        bands = jnp.broadcast_to(1.0 / own, (16, 128))
        whole = jnp.where(sub < 2, -jnp.broadcast_to(inverse[m : m + 1], (16, 128)), 0.0)
        weight[m] = jnp.concatenate([bands, bands, whole], 0) * (1.0 / (2.0 * (NBINS - 1)))
        index = index - 3 * ((index * 11) >> 5)
        for q in range(3):
            masks[m, q] = jnp.where(index == q, 1.0, 0.0).astype(BF)


def spread(place, held, rot_ref, turned, nat, sre, sim, delta):
    rc, rs = rot_ref[0], rot_ref[1]

    @pl.loop(0, 8)
    def _(k):
        a = place.member(delta, k)
        for q in range(4):
            re = held[a, pl.ds(32 * q, 32), :].astype(F32)
            im = held[a, pl.ds(ROWS_A + 32 * q, 32), :].astype(F32)
            tr = re * rc - im * rs
            ti = re * rs + im * rc
            turned[k, q] = tr.astype(BF)
            turned[k, 4 + q] = ti.astype(BF)
            nat[0, q, pl.ds(k * 32, 32), :] = tr
            nat[1, q, pl.ds(k * 32, 32), :] = ti

    for q in range(4):
        for c in range(32):
            sre[pl.ds(8 * q, 8), pl.ds(c * 128, 128)] = nat[0, q, pl.ds(c, 8, stride=32), :]
            sim[pl.ds(8 * q, 8), pl.ds(c * 128, 128)] = nat[1, q, pl.ds(c, 8, stride=32), :]


def requests(place, held, wanted, meta, sem, delta):
    shard = place.me.astype(F32)
    tiles = [held[place.member(delta, k), pl.ds(128, 16), :].astype(F32) for k in range(8)]
    rows = [jnp.concatenate([t[v : v + 1] for t in tiles], 0) for v in range(4)]
    lane = iota((8, 128), 1)
    hit = (rows[0] == shard) & (lane < 64)
    before = jnp.where(iota((128, 128), 0) < iota((128, 128), 1), 1.0, 0.0).astype(BF)
    rank = jnp.dot(jnp.where(hit, 1.0, 0.0).astype(BF), before, preferred_element_type=F32)
    table = jnp.zeros((8, 128), F32)
    for v in range(3):
        for k in range(4):
            value = jnp.sum(jnp.where(hit & (rank == float(k)), rows[v + 1], 0.0), axis=1, keepdims=True)
            table = jnp.where(lane == 4 * v + k, value, table)
    wanted[...] = table.astype(I32)
    copy = pltpu.make_async_copy(wanted, meta, sem)
    copy.start()
    return copy


def veto(w0_ref, far_ref, tn, meta, turned, masks, pick, weight, chi, slot, source):
    fc, fs = far_ref[0], far_ref[1]
    rows = []
    at = []
    for k in range(4):
        m = jnp.clip(meta[slot, k], 0, NT - 1)
        r = jnp.clip(meta[slot, 4 + k], 0, 1)
        blk = jnp.clip(meta[slot, 8 + k], 0, 1)
        at.append((m, blk))
        h0, h1 = tn[0, m], tn[1, m]
        sign = (2 * blk - 1).astype(F32).astype(BF)
        for d in range(2):
            re = turned[slot, 2 * d + r]
            im = turned[slot, 4 + 2 * d + r]
            xr = re * h0 + im * h1
            xi = (im * h0 - re * h1) * sign
            for q in range(3):
                mask = masks[m, q]
                rows.append(jnp.concatenate([xr * mask, xi * mask], 1))
    part = jnp.dot(jnp.concatenate(rows, 0), w0_ref[...], preferred_element_type=F32).astype(BF)
    lines = []
    for k in range(4):
        m, blk = at[k]
        turns = []
        for q in range(6):
            base = k * 192 + 32 * q
            ur = part[base : base + 32, :128]
            ui = part[base : base + 32, 128:]
            turns.append(jnp.concatenate([ur * fc - ui * fs, ur * fs + ui * fc], 1))
        bands = jnp.dot(pick[m], jnp.concatenate(turns, 0), preferred_element_type=F32)
        s = bands[:, :128] * bands[:, :128] + bands[:, 128:] * bands[:, 128:]
        lines.append((blk, jnp.sum(s * weight[m], axis=0, keepdims=True)))
    value = jnp.concatenate([line for _, line in lines] * 2, 0)
    back = jnp.take_along_axis(value, 127 - iota((8, 128), 1), axis=1)
    sub = iota((8, 128), 0) % 4
    late = jnp.zeros((8, 128), I32)
    for k in range(4):
        late = jnp.where(sub == k, lines[k][0], late)
    chi[source] = jnp.where(late == 1, value, back)


def filters(place, table_ref, tmf, itp, sre, sim, lhs, snr_ref, peak, delta, first):
    for n in range(4):
        for k in range(F // 256):
            cut = pl.ds(k * 256, 256)
            h0 = tmf[0, pl.ds(first + n, 1), cut]
            h1 = tmf[1, pl.ds(first + n, 1), cut]
            re = sre[:, cut]
            im = sim[:, cut]
            lhs[pl.ds(64 * n, 32), cut] = (re * h0 + im * h1).astype(BF)
            lhs[pl.ds(64 * n + 32, 32), cut] = (im * h0 - re * h1).astype(BF)
    acc = jnp.dot(lhs[...], table_ref[...], preferred_element_type=F32)
    back = 127 - iota((16, 128), 1)
    one = (place.y + delta) % 4 * 4
    two = 64 + (place.x + delta) % 4 * 16
    for n in range(4):
        a = acc[64 * n : 64 * n + 32, :128]
        d = acc[64 * n : 64 * n + 32, 128:]
        c = acc[64 * n + 32 : 64 * n + 64, :128]
        b = acc[64 * n + 32 : 64 * n + 64, 128:]
        plus = (a - b) * (a - b) + (c + d) * (c + d)
        minus = (a + b) * (a + b) + (c - d) * (c - d)
        scale = itp[pl.ds(first + n, 1), :]
        plus = (plus[:16] + plus[16:]) * scale
        minus = (minus[:16] + minus[16:]) * scale
        top = jnp.maximum(plus, minus)
        top = jnp.maximum(top[:8], top[8:])
        peak[first + n] = jnp.maximum(peak[first + n], top)
        minus = jnp.take_along_axis(minus, back, axis=1)
        for half, value in enumerate((minus, plus)):
            for r in range(2):
                to = 2 * half + r
                snr_ref[first + n, pl.ds(one + to, 4, stride=16), :] = value[8 * r : 8 * r + 4]
                for k in range(4):
                    line = value[8 * r + 4 + k : 8 * r + 5 + k]
                    snr_ref[first + n, pl.ds(two + to + 4 * k, 1), :] = line


def kernel(
    spec_in, own_in, tmpl_in, seg_in, blk_in, tm_in, bounds_in, rot_in, w0_in, far_in, table_in,
    snr_ref, loud_ref, out_ref,
    spec_ref, own_ref, tmpl_ref, seg_ref, blk_ref, tm_ref, bounds_ref, rot_ref, w0_ref, far_ref, table_ref,
    held, listed, tmf, tn, itp, masks, pick, weight, turned, nat, sre, sim, lhs, peak, wanted, meta,
    chi, slots, tops, peaks,
    full_sem, half_sem, recv_sem, meta_sem, chi_send, chi_recv, pair_send, pair_recv, in_sem,
):
    place = Torus(held, full_sem, half_sem, recv_sem)
    me, seg = place.me, place.seg
    barrier = pltpu.get_barrier_semaphore()
    given = (spec_in, own_in, tmpl_in, seg_in, blk_in, tm_in, bounds_in, rot_in, w0_in, far_in, table_in)
    kept = (spec_ref, own_ref, tmpl_ref, seg_ref, blk_ref, tm_ref, bounds_ref, rot_ref, w0_ref, far_ref, table_ref)
    inputs = [pltpu.make_async_copy(a, b, in_sem.at[n]) for n, (a, b) in enumerate(zip(given, kept))]
    for copy in inputs:
        copy.start()

    @pl.loop(1, 32)
    def _(j):
        pl.semaphore_signal(barrier, inc=1, device_id=((me + j) % 32, seg), device_id_type=MESH)

    for j in range(1, 4):
        pl.semaphore_signal(barrier, inc=1, device_id=(me, (seg + j) % 4), device_id_type=MESH)
    for copy in inputs[:5]:
        copy.wait()
    lay_out(spec_ref, own_ref, tmpl_ref, seg_ref, blk_ref, tm_ref, held, tn, nat, listed, me)
    pl.semaphore_wait(barrier, 34)
    place.begin()
    for copy in inputs[5:]:
        copy.wait()
    prepare(tm_ref, bounds_ref, tmf, tn, nat, itp, masks, pick, weight)
    peak[...] = jnp.zeros_like(peak)
    place.first()

    def result(source):
        return pltpu.make_async_remote_copy(
            src_ref=chi.at[source],
            dst_ref=slots.at[me],
            send_sem=chi_send.at[source],
            recv_sem=chi_recv.at[me],
            device_id=(source, seg),
            device_id_type=MESH,
        )

    def group(delta, between):
        asked = requests(place, held, wanted, meta, meta_sem, delta)
        spread(place, held, rot_ref, turned, nat, sre, sim, delta)
        asked.wait()

        @pl.loop(0, 2)
        def _(part):
            for n in range(4):
                slot = part * 4 + n
                source = place.member(delta, slot)
                veto(w0_ref, far_ref, tn, meta, turned, masks, pick, weight, chi, slot, source)

        @pl.loop(0, 8)
        def _(k):
            source = place.member(delta, k)

            @pl.when(source != me)
            def _():
                result(source).start()

        @pl.loop(0, 4)
        def _(step):
            filters(place, table_ref, tmf, itp, sre, sim, lhs, snr_ref, peak, delta, step * 4)
            if between is not None:
                between(step)

    group(0, lambda step: place.onward(step + step // 2 * (1 - 2 * (step % 2))))

    @pl.loop(0, 2)
    def _(n):
        group(1 + 2 * n, None)

    place.last()
    group(2, None)

    slots[pl.ds(me, 1)] = chi[pl.ds(me, 1)]
    tops[...] = jnp.concatenate([jnp.max(peak[m], axis=0, keepdims=True) for m in range(NT)], 0)
    pairs = [
        pltpu.make_async_remote_copy(
            src_ref=tops,
            dst_ref=peaks.at[j],
            send_sem=pair_send.at[j],
            recv_sem=pair_recv.at[j],
            device_id=(me, (seg + j) % 4),
            device_id_type=MESH,
        )
        for j in range(1, 4)
    ]
    for copy in pairs:
        copy.start()

    @pl.loop(0, 32)
    def _(other):
        @pl.when(other != me)
        def _():
            pltpu.make_async_remote_copy(
                src_ref=chi.at[other],
                dst_ref=slots.at[other],
                send_sem=chi_send.at[other],
                recv_sem=chi_recv.at[other],
                device_id=(other, seg),
                device_id_type=MESH,
            ).wait()

    i, j = iota((64, 64), 0), iota((64, 64), 1)
    across = own_ref[...]
    owner = jnp.sum(jnp.where(i == j, across, 0), axis=1, keepdims=True)
    rank = jnp.sum(jnp.where((j < i) & (across == owner), 1, 0), axis=1, keepdims=True)
    choose = jnp.where(iota((64, 256), 1) == owner * 8 + rank, 1.0, 0.0)
    out_ref[...] = jnp.dot(
        choose, slots[...].reshape(256, 128), preferred_element_type=F32, precision=lax.Precision.HIGHEST
    )
    place.finish()
    for copy in pairs:
        copy.wait()
    top = jnp.maximum(jnp.maximum(tops[...], peaks[1]), jnp.maximum(peaks[2], peaks[3]))
    top = jnp.max(top, axis=1, keepdims=True)
    loud = jnp.max(jnp.where(iota((NT, 128), 0) == iota((NT, 128), 1), top, 0.0), axis=0, keepdims=True)
    loud_ref[...] = loud[:, :NT]


def body(
    spectra, templates, bounds, trigger_owner, trigger_template, trigger_segment, trigger_block
):
    vmem = pl.BlockSpec(memory_space=pltpu.VMEM)
    dma = pltpu.SemaphoreType.DMA
    wave, rot, w0, far = tables()
    snr, loud, chisq = pl.pallas_call(
        kernel,
        out_shape=(
            jax.ShapeDtypeStruct((NT, 128, 128), F32),
            jax.ShapeDtypeStruct((1, NT), F32),
            jax.ShapeDtypeStruct((64, 128), F32),
        ),
        in_specs=[pl.BlockSpec(memory_space=pltpu.HBM)] * 11,
        out_specs=(vmem, vmem, vmem),
        scratch_shapes=[
            pltpu.VMEM((2, 2, 2, F), BF),
            pltpu.VMEM((1, 64), I32),
            pltpu.VMEM((1, 64), I32),
            pltpu.VMEM((1, 64), I32),
            pltpu.VMEM((1, 64), I32),
            pltpu.VMEM((2, NT, F), BF),
            pltpu.SMEM((NT, 15), I32),
            pltpu.VMEM((2, 32, 128), F32),
            pltpu.VMEM((256, 256), BF),
            pltpu.VMEM((2, 32, 128), BF),
            pltpu.VMEM((F, 256), BF),
            pltpu.VMEM((32, ROWS, 128), BF),
            pltpu.VMEM((16, 128), F32),
            pltpu.VMEM((2, NT, F), F32),
            pltpu.VMEM((2, NT, 32, 128), BF),
            pltpu.VMEM((NT, 128), F32),
            pltpu.VMEM((NT, 3, 32, 128), BF),
            pltpu.VMEM((NT, 48, 192), BF),
            pltpu.VMEM((NT, 48, 128), F32),
            pltpu.VMEM((8, 8, 32, 128), BF),
            pltpu.VMEM((2, 4, 288, 128), F32),
            pltpu.VMEM((32, F), F32),
            pltpu.VMEM((32, F), F32),
            pltpu.VMEM((256, F), BF),
            pltpu.VMEM((NT, 8, 128), F32),
            pltpu.VMEM((8, 128), I32),
            pltpu.SMEM((8, 128), I32),
            pltpu.VMEM((32, 8, 128), F32),
            pltpu.VMEM((32, 8, 128), F32),
            pltpu.VMEM((NT, 128), F32),
            pltpu.VMEM((4, NT, 128), F32),
            dma((21,)),
            dma((2, 10)),
            dma((2, 32)),
            dma,
            dma((32,)),
            dma((32,)),
            dma((4,)),
            dma((4,)),
            dma((11,)),
        ],
        compiler_params=pltpu.CompilerParams(
            collective_id=0, has_side_effects=True, vmem_limit_bytes=62 * 1024 * 1024
        ),
        name="search",
    )(
        spectra.reshape(2, 2, 2, F),
        trigger_owner.reshape(1, 64),
        trigger_template.reshape(1, 64),
        trigger_segment.reshape(1, 64),
        trigger_block.reshape(1, 64),
        templates,
        bounds,
        rot,
        w0,
        far,
        wave,
    )
    snr = snr.reshape(NT, 32, 2, 2, 128).transpose(0, 1, 3, 2, 4).reshape(NT, 32, 2, 256)
    return snr, loud.reshape(NT), chisq


def solution(mesh):
    in_specs = (
        P(None, None, "tmpl", "seg", None),
        P(None, "tmpl", None),
        P("tmpl", None),
        P(("tmpl", "seg"), None),
        P(("tmpl", "seg")),
        P(("tmpl", "seg")),
        P(("tmpl", "seg")),
    )
    out_specs = (P("tmpl", None, "seg", None), P("tmpl"), P(("tmpl", "seg"), None))
    return jax.shard_map(body, mesh=mesh, in_specs=in_specs, out_specs=out_specs, check_vma=False)
```

```python
import math

import jax
import jax.numpy as jnp
import numpy as np
from jax import lax
from jax.experimental import pallas as pl
from jax.experimental.pallas import tpu as pltpu
from jax.sharding import PartitionSpec as P

F = 4096
NT = 16
NBINS = 16
EPSILON = 1e-06
BF = jnp.bfloat16
F32 = jnp.float32
I32 = jnp.int32
MESH = pl.DeviceIdType.MESH
ROWS_A = 144
ROWS = 272


def tables():
    step = 2.0 * math.pi / 4096.0
    phi = np.arange(4096, dtype=np.float64) - 2048.0
    half = np.arange(128, dtype=np.float64) + 0.5
    ang = step * phi[:, None] * half[None, :]
    main = np.concatenate([np.cos(ang), np.sin(ang)], 1)
    turn = (step * 127.5 * phi).reshape(32, 128)
    rot = np.stack([np.cos(turn), np.sin(turn)])
    near = step * np.arange(128.0)[:, None] * half[None, :]
    w0 = np.concatenate(
        [
            np.concatenate([np.cos(near), np.sin(near)], 1),
            np.concatenate([-np.sin(near), np.cos(near)], 1),
        ],
        0,
    )
    far = step * (128.0 * np.arange(32.0) - 2048.0)[:, None] * half[None, :]
    far = np.stack([np.cos(far), np.sin(far)])
    return (
        jnp.asarray(main, F32).astype(BF),
        jnp.asarray(rot, F32),
        jnp.asarray(w0, F32).astype(BF),
        jnp.asarray(far, F32).astype(BF),
    )


def iota(shape, dim):
    return lax.broadcasted_iota(I32, shape, dim)


def ring(zz, xx, yy):
    return zz * 16 + xx % 4 * 4 + yy % 4


class Torus:
    def __init__(self, held, full_sem, half_sem, recv_sem):
        self.me = lax.axis_index("tmpl")
        self.seg = lax.axis_index("seg")
        self.z, self.x, self.y = self.me // 16, self.me // 4 % 4, self.me % 4
        self.held, self.full_sem, self.half_sem, self.recv_sem = held, full_sem, half_sem, recv_sem

    def step(self, kind, near, far, here=False):
        plane = self.z if kind == 0 else 1 - self.z
        xx = self.x + near * (1 - plane) + far * plane
        yy = self.y + near * plane + far * (1 - plane)
        return ring(self.z if here else plane, xx, yy)

    def member(self, delta, k):
        plane, at = k // 4, k % 4
        first = at * 4 + (self.y + delta) % 4
        second = 16 + (self.x + delta) % 4 * 4 + at
        return (1 - plane) * first + plane * second

    def copy(self, source, peer, half, sem):
        if half is None:
            view, recv, send = self.held.at[source], self.recv_sem.at[0, source], self.full_sem.at[sem]
        else:
            cut = pl.ds(0, ROWS_A) if half == 0 else pl.ds(ROWS_A, ROWS - ROWS_A)
            view, recv, send = self.held.at[source, cut], self.recv_sem.at[half, source], self.half_sem.at[half, sem]
        return pltpu.make_async_remote_copy(
            src_ref=view, dst_ref=view, send_sem=send, recv_sem=recv, device_id=(peer, self.seg), device_id_type=MESH
        )

    def arrive(self, source, halves=False):
        peer = ring(1 - self.z, self.x, self.y)
        for half in (0, 1) if halves else (None,):
            self.copy(source, peer, half, 0).wait_recv()

    def fan(self, kind, near):
        source = self.step(kind, near, 0)
        for n, far in enumerate((1, 3)):
            self.copy(source, self.step(kind, 0, far, True), None, 5 + kind * 8 + near * 2 + n).start()

    def sides(self, kind):
        source = self.step(kind, 0, 0)
        for n, near in enumerate((1, 3)):
            self.copy(source, self.step(kind, near, 0, True), None, 1 + kind * 2 + n).start()

    def begin(self):
        mate = ring(1 - self.z, self.x, self.y)
        self.copy(self.me, mate, None, 0).start()
        self.sides(0)
        self.fan(0, 0)

    def place_of(self, source):
        plane = source // 16
        return plane * (4 + source % 4) + (1 - plane) * (source // 4 % 4)

    def first(self, work):
        mate = self.step(1, 0, 0)
        self.arrive(mate)
        self.sides(1)
        work([self.me, mate])
        for kind in (0, 1):
            for near in (1, 3):
                source = self.step(kind, near, 0)
                self.arrive(source)
                self.copy(source, self.step(kind, 4 - near, 0, True), 1 if near == 1 else 0, kind).start()
            if kind == 0:
                self.fan(1, 0)
        for kind in (0, 1):
            for near in (1, 3):
                self.fan(kind, near)
        work([self.step(kind, near, 0) for kind in (0, 1) for near in (1, 3)])
        for kind in (0, 1):
            self.arrive(self.step(kind, 2, 0), True)
            self.fan(kind, 2)
        work([self.step(kind, 2, 0) for kind in (0, 1)])

    def onward(self, near):
        for kind in (0, 1):
            for far in (1, 3):
                source = self.step(kind, near, far)
                self.arrive(source)
                self.copy(source, self.step(kind, 0, 4 - far, True), 1 if far == 1 else 0, 2 + kind * 4 + near).start()

    def last(self):
        @pl.loop(0, 4)
        def _(near):
            for kind in (0, 1):
                self.arrive(self.step(kind, near, 2), True)

    def finish(self):
        peer = ring(1 - self.z, self.x, self.y)

        @pl.loop(0, 21)
        def _(n):
            self.copy(self.me, peer, None, n).wait_send()

        @pl.loop(0, 10)
        def _(n):
            for half in (0, 1):
                self.copy(self.me, peer, half, n).wait_send()


def lay_out(spec_ref, own_ref, tmpl_ref, seg_ref, blk_ref, tm_ref, held, tn, nat, listed, me):
    listed[...] = jnp.zeros_like(listed)
    for v, ref in enumerate((own_ref, tmpl_ref, seg_ref, blk_ref)):
        listed[pl.ds(v, 1), pl.ds(0, 64)] = ref[...].astype(F32)
    held[me, pl.ds(128, 16), :] = listed[...].astype(BF)
    for p in range(2):
        for d in range(2):
            value = spec_ref[p, d].astype(F32)
            for c in range(32):
                nat[p, d, pl.ds(c, 2, stride=32), :] = value[:, 128 * c : 128 * c + 128]
    for p in range(2):
        for d in range(2):
            held[me, pl.ds(p * ROWS_A + 64 * d, 64), :] = nat[p, d, pl.ds(0, 64), :].astype(BF)


def prepare(tm_ref, bounds_ref, tmf, tn, nat, itp, masks, pick, weight):
    lane = iota((16, 128), 1)
    sub = iota((16, 128), 0)
    quarter, chunk = lane // 32, lane % 32
    cls = sub % 3
    natural = iota((32, 128), 0) * 128 + iota((32, 128), 1)
    freq = iota((16, F), 1)
    h0 = tm_ref[0].astype(F32)
    h1 = tm_ref[1].astype(F32)
    tmf[0] = h0
    tmf[1] = h1
    for p in range(2):
        for h in range(2):
            for c in range(32):
                nat[p, h, pl.ds(c, 8, stride=32), :] = tmf[p, pl.ds(8 * h, 8), pl.ds(128 * c, 128)]
            for m in range(8):
                tn[p, 8 * h + m] = nat[p, h, pl.ds(32 * m, 32), :].astype(BF)
    energy = h0 * h0 + h1 * h1
    rows16 = iota((16, 1), 0)

    def column(l):
        col = jnp.zeros((16, 1), I32)
        for m in range(NT):
            col = jnp.where(rows16 == m, bounds_ref[m, l], col)
        return col

    edges = [jnp.zeros((16, 1), I32)] + [column(l) for l in range(15)] + [jnp.full((16, 1), F, I32)]
    total = jnp.zeros((16, 1), F32)
    powers = jnp.zeros((16, 128), F32)
    for l in range(NBINS):
        inside = (freq >= edges[l]) & (freq < edges[l + 1])
        band = jnp.sum(jnp.where(inside, energy, 0.0), axis=1, keepdims=True) + EPSILON
        total = total + band
        powers = jnp.where(lane == l, band, powers)
    inverse = jnp.broadcast_to(1.0 / total, (16, 128))
    itp[...] = inverse
    none = jnp.zeros((16, 96), F32)
    short = iota((16, 96), 0)
    sums = jnp.concatenate([jnp.where(short == 0, 1.0, none), jnp.where(short == 1, 1.0, none)], 1)
    for m in range(NT):
        low = jnp.zeros((16, 128), I32)
        high = jnp.full((16, 128), F, I32)
        index = jnp.zeros((32, 128), I32)
        for l in range(15):
            edge = bounds_ref[m, l]
            low = jnp.where(sub == l + 1, edge, low)
            high = jnp.where(sub == l, edge, high)
            index = index + jnp.where(natural >= edge, 1, 0)
        touch = (cls == quarter) & (low < 128 * chunk + 128) & (high > 128 * chunk)
        touch = jnp.where(touch, 1.0, 0.0)[:, :96]
        pick[m] = jnp.concatenate(
            [jnp.concatenate([touch, none], 1), jnp.concatenate([none, touch], 1), sums], 0
        ).astype(BF)
        own = jnp.where(sub == lane, jnp.broadcast_to(powers[m : m + 1], (16, 128)), 0.0)
        own = jnp.sum(own, axis=1, keepdims=True)
        bands = jnp.broadcast_to(1.0 / own, (16, 128))
        whole = jnp.where(sub < 2, -jnp.broadcast_to(inverse[m : m + 1], (16, 128)), 0.0)
        weight[m] = jnp.concatenate([bands, bands, whole], 0) * (1.0 / (2.0 * (NBINS - 1)))
        index = index - 3 * ((index * 11) >> 5)
        for q in range(3):
            masks[m, q] = jnp.where(index == q, 1.0, 0.0).astype(BF)


def turn(held, rot_ref, turned, nat, source, k):
    rc, rs = rot_ref[0], rot_ref[1]
    for q in range(4):
        re = held[source, pl.ds(32 * q, 32), :].astype(F32)
        im = held[source, pl.ds(ROWS_A + 32 * q, 32), :].astype(F32)
        tr = re * rc - im * rs
        ti = re * rs + im * rc
        turned[k, q] = tr.astype(BF)
        turned[k, 4 + q] = ti.astype(BF)
        nat[0, q, pl.ds(pl.multiple_of(k * 32, 32), 32), :] = tr
        nat[1, q, pl.ds(pl.multiple_of(k * 32, 32), 32), :] = ti


def spread(nat, sre, sim):
    for q in range(4):
        for c in range(32):
            sre[pl.ds(8 * q, 8), pl.ds(c * 128, 128)] = nat[0, q, pl.ds(c, 8, stride=32), :]
            sim[pl.ds(8 * q, 8), pl.ds(c * 128, 128)] = nat[1, q, pl.ds(c, 8, stride=32), :]


def requests(place, held, wanted, meta, sem, sources):
    shard = place.me.astype(F32)
    tiles = [held[source, pl.ds(128, 16), :].astype(F32) for source in sources]
    tiles = tiles + tiles[:1] * (8 - len(tiles))
    rows = [jnp.concatenate([t[v : v + 1] for t in tiles], 0) for v in range(4)]
    lane = iota((8, 128), 1)
    hit = (rows[0] == shard) & (lane < 64)
    before = jnp.where(iota((128, 128), 0) < iota((128, 128), 1), 1.0, 0.0).astype(BF)
    rank = jnp.dot(jnp.where(hit, 1.0, 0.0).astype(BF), before, preferred_element_type=F32)
    terms = [jnp.where(hit & (rank == float(k)), rows[v + 1], 0.0) for v in range(3) for k in range(4)]
    sums = jnp.dot(jnp.concatenate(terms, 0).astype(BF), jnp.ones((128, 128), BF), preferred_element_type=F32)
    table = jnp.zeros((8, 128), F32)
    for n in range(12):
        table = jnp.where(lane == n, sums[8 * n : 8 * n + 8], table)
    wanted[...] = table.astype(I32)
    copy = pltpu.make_async_copy(wanted, meta, sem)
    copy.start()
    return copy


def veto(w0_ref, far_ref, tn, meta, turned, masks, pick, weight, chi, row, slot, source):
    fc, fs = far_ref[0], far_ref[1]
    rows = []
    at = []
    for k in range(4):
        m = jnp.clip(meta[row, k], 0, NT - 1)
        r = jnp.clip(meta[row, 4 + k], 0, 1)
        blk = jnp.clip(meta[row, 8 + k], 0, 1)
        at.append((m, blk))
        h0, h1 = tn[0, m], tn[1, m]
        sign = (2 * blk - 1).astype(F32).astype(BF)
        for d in range(2):
            re = turned[slot, 2 * d + r]
            im = turned[slot, 4 + 2 * d + r]
            xr = re * h0 + im * h1
            xi = (im * h0 - re * h1) * sign
            for q in range(3):
                mask = masks[m, q]
                rows.append(jnp.concatenate([xr * mask, xi * mask], 1))
    part = jnp.dot(jnp.concatenate(rows, 0), w0_ref[...], preferred_element_type=F32).astype(BF)
    lines = []
    for k in range(4):
        m, blk = at[k]
        turns = []
        for q in range(6):
            base = k * 192 + 32 * q
            ur = part[base : base + 32, :128]
            ui = part[base : base + 32, 128:]
            turns.append(jnp.concatenate([ur * fc - ui * fs, ur * fs + ui * fc], 1))
        bands = jnp.dot(pick[m], jnp.concatenate(turns, 0), preferred_element_type=F32)
        s = bands[:, :128] * bands[:, :128] + bands[:, 128:] * bands[:, 128:]
        lines.append((blk, jnp.sum(s * weight[m], axis=0, keepdims=True)))
    value = jnp.concatenate([line for _, line in lines] * 2, 0)
    back = jnp.take_along_axis(value, 127 - iota((8, 128), 1), axis=1)
    sub = iota((8, 128), 0) % 4
    late = jnp.zeros((8, 128), I32)
    for k in range(4):
        late = jnp.where(sub == k, lines[k][0], late)
    chi[source // 4 % 4, source // 16, source % 4] = jnp.where(late == 1, value, back)


def filters(place, table_ref, tmf, itp, sre, sim, lhs, snr_ref, peak, delta, first):
    for n in range(4):
        for k in range(F // 256):
            cut = pl.ds(k * 256, 256)
            h0 = tmf[0, pl.ds(first + n, 1), cut]
            h1 = tmf[1, pl.ds(first + n, 1), cut]
            re = sre[:, cut]
            im = sim[:, cut]
            lhs[pl.ds(64 * n, 32), cut] = (re * h0 + im * h1).astype(BF)
            lhs[pl.ds(64 * n + 32, 32), cut] = (im * h0 - re * h1).astype(BF)
    acc = jnp.dot(lhs[...], table_ref[...], preferred_element_type=F32)
    back = 127 - iota((16, 128), 1)
    one = (place.y + delta) % 4 * 4
    two = 64 + (place.x + delta) % 4 * 16
    for n in range(4):
        a = acc[64 * n : 64 * n + 32, :128]
        d = acc[64 * n : 64 * n + 32, 128:]
        c = acc[64 * n + 32 : 64 * n + 64, :128]
        b = acc[64 * n + 32 : 64 * n + 64, 128:]
        plus = (a - b) * (a - b) + (c + d) * (c + d)
        minus = (a + b) * (a + b) + (c - d) * (c - d)
        scale = itp[pl.ds(first + n, 1), :]
        plus = (plus[:16] + plus[16:]) * scale
        minus = (minus[:16] + minus[16:]) * scale
        top = jnp.maximum(plus, minus)
        top = jnp.maximum(top[:8], top[8:])
        peak[first + n] = jnp.maximum(peak[first + n], top)
        minus = jnp.take_along_axis(minus, back, axis=1)
        for half, value in enumerate((minus, plus)):
            for r in range(2):
                to = 2 * half + r
                snr_ref[first + n, pl.ds(one + to, 4, stride=16), :] = value[8 * r : 8 * r + 4]
                for k in range(4):
                    line = value[8 * r + 4 + k : 8 * r + 5 + k]
                    snr_ref[first + n, pl.ds(two + to + 4 * k, 1), :] = line


def kernel(
    spec_in, own_in, tmpl_in, seg_in, blk_in, tm_in, bounds_in, rot_in, w0_in, far_in, table_in,
    snr_ref, loud_ref, out_ref,
    spec_ref, own_ref, tmpl_ref, seg_ref, blk_ref, tm_ref, bounds_ref, rot_ref, w0_ref, far_ref, table_ref,
    held, listed, tmf, tn, itp, masks, pick, weight, turned, nat, sre, sim, lhs, peak, wanted, meta,
    chi, over_x, over_y, slots, tops, peaks,
    full_sem, half_sem, recv_sem, meta_sem, chi_send, chi_recv, pair_send, pair_recv, in_sem,
):
    place = Torus(held, full_sem, half_sem, recv_sem)
    me, seg = place.me, place.seg
    barrier = pltpu.get_barrier_semaphore()
    given = (spec_in, own_in, tmpl_in, seg_in, blk_in, tm_in, bounds_in, rot_in, w0_in, far_in, table_in)
    kept = (spec_ref, own_ref, tmpl_ref, seg_ref, blk_ref, tm_ref, bounds_ref, rot_ref, w0_ref, far_ref, table_ref)
    inputs = [pltpu.make_async_copy(a, b, in_sem.at[n]) for n, (a, b) in enumerate(zip(given, kept))]
    for copy in inputs:
        copy.start()

    z, x, y = place.z, place.x, place.y
    friends = [(ring(1 - z, x, y), seg)]
    for j in (1, 3, 2):
        friends += [(ring(z, x + j, y), seg), (ring(z, x, y + j), seg)]
    friends += [(me, (seg + j) % 4) for j in range(1, 4)]
    for friend in friends:
        pl.semaphore_signal(barrier, inc=1, device_id=friend, device_id_type=MESH)
    for copy in inputs[:5]:
        copy.wait()
    lay_out(spec_ref, own_ref, tmpl_ref, seg_ref, blk_ref, tm_ref, held, tn, nat, listed, me)
    pl.semaphore_wait(barrier, 10)
    place.begin()
    for copy in inputs[5:]:
        copy.wait()
    prepare(tm_ref, bounds_ref, tmf, tn, nat, itp, masks, pick, weight)
    peak[...] = jnp.zeros_like(peak)

    def work(sources):
        asked = requests(place, held, wanted, meta, meta_sem, sources)
        for source in sources:
            turn(held, rot_ref, turned, nat, source, place.place_of(source))
        asked.wait()
        for row, source in enumerate(sources):
            veto(w0_ref, far_ref, tn, meta, turned, masks, pick, weight, chi, row, place.place_of(source), source)

    def serve(delta):
        asked = requests(place, held, wanted, meta, meta_sem, [place.member(delta, k) for k in range(8)])

        @pl.loop(0, 8)
        def _(k):
            turn(held, rot_ref, turned, nat, place.member(delta, k), k)

        asked.wait()

        @pl.loop(0, 2)
        def _(part):
            for n in range(4):
                slot = part * 4 + n
                source = place.member(delta, slot)
                veto(w0_ref, far_ref, tn, meta, turned, masks, pick, weight, chi, slot, slot, source)

    def scan(delta, between):
        spread(nat, sre, sim)

        @pl.loop(0, 4)
        def _(step):
            filters(place, table_ref, tmf, itp, sre, sim, lhs, snr_ref, peak, delta, step * 4)
            if between is not None:
                between(step)

    def result(axis, j):
        if axis == 0:
            src, dst, peer = chi.at[(x + j) % 4], over_x.at[x], ring(z, x + j, y)
        elif axis == 1:
            src, dst, peer = over_x.at[:, :, (y + j) % 4], over_y.at[y], ring(z, x, y + j)
        else:
            src, dst, peer = over_y.at[:, :, 1 - z], slots.at[z], ring(1 - z, x, y)
        return pltpu.make_async_remote_copy(
            src_ref=src,
            dst_ref=dst,
            send_sem=chi_send.at[axis, j],
            recv_sem=chi_recv.at[axis, j],
            device_id=(peer, seg),
            device_id_type=MESH,
        )

    place.first(work)
    scan(0, lambda step: place.onward(step + step // 2 * (1 - 2 * (step % 2))))

    @pl.loop(0, 2)
    def _(n):
        serve(1 + 2 * n)
        scan(1 + 2 * n, None)

    place.last()
    serve(2)
    for j in (1, 2, 3):
        result(0, j).start()
    over_x[pl.ds(x, 1)] = chi[pl.ds(x, 1)]

    def homeward(step):
        @pl.when(step == 1)
        def _():
            for j in (1, 2, 3):
                result(0, j).wait()
            for j in (1, 2, 3):
                result(1, j).start()
            for n in range(4):
                for p in range(2):
                    over_y[y, n, p] = over_x[n, p, y]

        @pl.when(step == 3)
        def _():
            for j in (1, 2, 3):
                result(1, j).wait()
            result(2, 0).start()
            for n in range(4):
                for p in range(4):
                    slots[z, n, p] = over_y[n, p, z]

    scan(2, homeward)
    tops[...] = jnp.concatenate([jnp.max(peak[m], axis=0, keepdims=True) for m in range(NT)], 0)
    pairs = [
        pltpu.make_async_remote_copy(
            src_ref=tops,
            dst_ref=peaks.at[j],
            send_sem=pair_send.at[j],
            recv_sem=pair_recv.at[j],
            device_id=(me, (seg + j) % 4),
            device_id_type=MESH,
        )
        for j in range(1, 4)
    ]
    for copy in pairs:
        copy.start()
    place.finish()
    result(2, 0).wait()
    i, j = iota((64, 64), 0), iota((64, 64), 1)
    across = own_ref[...]
    owner = jnp.sum(jnp.where(i == j, across, 0), axis=1, keepdims=True)
    rank = jnp.sum(jnp.where((j < i) & (across == owner), 1, 0), axis=1, keepdims=True)
    where = owner // 16 * 16 + owner % 4 * 4 + owner // 4 % 4
    choose = jnp.where(iota((64, 256), 1) == where * 8 + rank, 1.0, 0.0)
    out_ref[...] = jnp.dot(
        choose, slots[...].reshape(256, 128), preferred_element_type=F32, precision=lax.Precision.HIGHEST
    )
    for copy in pairs:
        copy.wait()
    top = jnp.maximum(jnp.maximum(tops[...], peaks[1]), jnp.maximum(peaks[2], peaks[3]))
    top = jnp.max(top, axis=1, keepdims=True)
    loud = jnp.max(jnp.where(iota((NT, 128), 0) == iota((NT, 128), 1), top, 0.0), axis=0, keepdims=True)
    loud_ref[...] = loud[:, :NT]


def handed_kernel(*refs):
    sem = refs[6]
    copies = [pltpu.make_async_copy(refs[n], refs[n + 3], sem.at[n]) for n in (1, 2)]
    for n in range(4):
        cut = pl.ds(4 * n, 4)
        copies.append(pltpu.make_async_copy(refs[0].at[cut], refs[3].at[cut], sem.at[3 + n]))
    for copy in copies:
        copy.start()
    for copy in copies:
        copy.wait()


def handed(*arrays):
    hbm = pl.BlockSpec(memory_space=pltpu.HBM)
    return pl.pallas_call(
        handed_kernel,
        out_shape=tuple(jax.ShapeDtypeStruct(a.shape, a.dtype) for a in arrays),
        in_specs=[hbm] * 3,
        out_specs=(hbm,) * 3,
        scratch_shapes=[pltpu.SemaphoreType.DMA((7,))],
        name="handed",
    )(*arrays)


def body(
    spectra, templates, bounds, trigger_owner, trigger_template, trigger_segment, trigger_block
):
    vmem = pl.BlockSpec(memory_space=pltpu.VMEM)
    dma = pltpu.SemaphoreType.DMA
    wave, rot, w0, far = tables()
    snr, loud, chisq = pl.pallas_call(
        kernel,
        out_shape=(
            jax.ShapeDtypeStruct((NT, 128, 128), F32),
            jax.ShapeDtypeStruct((1, NT), F32),
            jax.ShapeDtypeStruct((64, 128), F32),
        ),
        in_specs=[pl.BlockSpec(memory_space=pltpu.HBM)] * 11,
        out_specs=(vmem, vmem, vmem),
        scratch_shapes=[
            pltpu.VMEM((2, 2, 2, F), BF),
            pltpu.VMEM((1, 64), I32),
            pltpu.VMEM((1, 64), I32),
            pltpu.VMEM((1, 64), I32),
            pltpu.VMEM((1, 64), I32),
            pltpu.VMEM((2, NT, F), BF),
            pltpu.SMEM((NT, 15), I32),
            pltpu.VMEM((2, 32, 128), F32),
            pltpu.VMEM((256, 256), BF),
            pltpu.VMEM((2, 32, 128), BF),
            pltpu.VMEM((F, 256), BF),
            pltpu.VMEM((32, ROWS, 128), BF),
            pltpu.VMEM((16, 128), F32),
            pltpu.VMEM((2, NT, F), F32),
            pltpu.VMEM((2, NT, 32, 128), BF),
            pltpu.VMEM((NT, 128), F32),
            pltpu.VMEM((NT, 3, 32, 128), BF),
            pltpu.VMEM((NT, 48, 192), BF),
            pltpu.VMEM((NT, 48, 128), F32),
            pltpu.VMEM((8, 8, 32, 128), BF),
            pltpu.VMEM((2, 4, 288, 128), F32),
            pltpu.VMEM((32, F), F32),
            pltpu.VMEM((32, F), F32),
            pltpu.VMEM((256, F), BF),
            pltpu.VMEM((NT, 8, 128), F32),
            pltpu.VMEM((8, 128), I32),
            pltpu.SMEM((8, 128), I32),
            pltpu.VMEM((4, 2, 4, 8, 128), F32),
            pltpu.VMEM((4, 2, 4, 8, 128), F32),
            pltpu.VMEM((4, 4, 2, 8, 128), F32),
            pltpu.VMEM((2, 4, 4, 8, 128), F32),
            pltpu.VMEM((NT, 128), F32),
            pltpu.VMEM((4, NT, 128), F32),
            dma((21,)),
            dma((2, 10)),
            dma((2, 32)),
            dma,
            dma((3, 4)),
            dma((3, 4)),
            dma((4,)),
            dma((4,)),
            dma((11,)),
        ],
        compiler_params=pltpu.CompilerParams(
            collective_id=0, has_side_effects=True, vmem_limit_bytes=62 * 1024 * 1024
        ),
        name="search",
    )(
        spectra.reshape(2, 2, 2, F),
        trigger_owner.reshape(1, 64),
        trigger_template.reshape(1, 64),
        trigger_segment.reshape(1, 64),
        trigger_block.reshape(1, 64),
        templates,
        bounds,
        rot,
        w0,
        far,
        wave,
    )
    snr, loud, chisq = handed(snr, loud, chisq)
    snr = snr.reshape(NT, 32, 2, 2, 128).transpose(0, 1, 3, 2, 4).reshape(NT, 32, 2, 256)
    return snr, loud.reshape(NT), chisq


def solution(mesh):
    in_specs = (
        P(None, None, "tmpl", "seg", None),
        P(None, "tmpl", None),
        P("tmpl", None),
        P(("tmpl", "seg"), None),
        P(("tmpl", "seg")),
        P(("tmpl", "seg")),
        P(("tmpl", "seg")),
    )
    out_specs = (P("tmpl", None, "seg", None), P("tmpl"), P(("tmpl", "seg"), None))
    return jax.shard_map(body, mesh=mesh, in_specs=in_specs, out_specs=out_specs, check_vma=False)
```

```python
import math

import jax
import jax.numpy as jnp
import numpy as np
from jax import lax
from jax.experimental import pallas as pl
from jax.experimental.pallas import tpu as pltpu
from jax.sharding import PartitionSpec as P

F = 4096
NT = 16
NBINS = 16
EPSILON = 1e-06
BF = jnp.bfloat16
F32 = jnp.float32
I32 = jnp.int32
MESH = pl.DeviceIdType.MESH
ROWS_A = 144
ROWS = 272


def tables():
    step = 2.0 * math.pi / 4096.0
    phi = np.arange(4096, dtype=np.float64) - 2048.0
    half = np.arange(128, dtype=np.float64) + 0.5
    ang = step * phi[:, None] * half[None, :]
    main = np.concatenate([np.cos(ang), np.sin(ang)], 1)
    turn = (step * 127.5 * phi).reshape(32, 128)
    rot = np.stack([np.cos(turn), np.sin(turn)])
    near = step * np.arange(128.0)[:, None] * half[None, :]
    w0 = np.concatenate(
        [
            np.concatenate([np.cos(near), np.sin(near)], 1),
            np.concatenate([-np.sin(near), np.cos(near)], 1),
        ],
        0,
    )
    far = step * (128.0 * np.arange(32.0) - 2048.0)[:, None] * half[None, :]
    far = np.stack([np.cos(far), np.sin(far)])
    return (
        jnp.asarray(main, F32).astype(BF),
        jnp.asarray(rot, F32),
        jnp.asarray(w0, F32).astype(BF),
        jnp.asarray(far, F32).astype(BF),
    )


def iota(shape, dim):
    return lax.broadcasted_iota(I32, shape, dim)


def ring(zz, xx, yy):
    return zz * 16 + xx % 4 * 4 + yy % 4


class Torus:
    def __init__(self, held, full_sem, half_sem, recv_sem):
        self.me = lax.axis_index("tmpl")
        self.seg = lax.axis_index("seg")
        self.z, self.x, self.y = self.me // 16, self.me // 4 % 4, self.me % 4
        self.held, self.full_sem, self.half_sem, self.recv_sem = held, full_sem, half_sem, recv_sem

    def step(self, kind, near, far, here=False):
        plane = self.z * (1 - kind) + (1 - self.z) * kind
        xx = self.x + near * (1 - plane) + far * plane
        yy = self.y + near * plane + far * (1 - plane)
        return ring(self.z if here else plane, xx, yy)

    def early(self, k):
        plane, at = k // 4, k % 4
        return (1 - plane) * (at * 4 + self.y) + plane * (16 + self.x * 4 + at)

    def beside(self, part, k):
        one = k // 2 % 2
        return self.step(k // 4, part * (3 - one) + (1 - part) * one, 1 + 2 * (k % 2))

    def across(self, k):
        return self.step(k // 4, k % 4, 2)

    def copy(self, source, peer, half, sem):
        if half is None:
            view, recv, send = self.held.at[source], self.recv_sem.at[0, source], self.full_sem.at[sem]
        else:
            cut = pl.ds(0, ROWS_A) if half == 0 else pl.ds(ROWS_A, ROWS - ROWS_A)
            view, recv, send = self.held.at[source, cut], self.recv_sem.at[half, source], self.half_sem.at[half, sem]
        return pltpu.make_async_remote_copy(
            src_ref=view, dst_ref=view, send_sem=send, recv_sem=recv, device_id=(peer, self.seg), device_id_type=MESH
        )

    def arrive(self, source, halves=False):
        peer = ring(1 - self.z, self.x, self.y)
        for half in (0, 1) if halves else (None,):
            self.copy(source, peer, half, 0).wait_recv()

    def fan(self, kind, near):
        source = self.step(kind, near, 0)
        for n, far in enumerate((1, 3)):
            self.copy(source, self.step(kind, 0, far, True), None, 5 + kind * 8 + near * 2 + n).start()

    def sides(self, kind):
        source = self.step(kind, 0, 0)
        for n, near in enumerate((1, 3)):
            self.copy(source, self.step(kind, near, 0, True), None, 1 + kind * 2 + n).start()

    def begin(self):
        mate = ring(1 - self.z, self.x, self.y)
        self.copy(self.me, mate, None, 0).start()
        self.sides(0)
        self.fan(0, 0)

    def place_of(self, source):
        plane = source // 16
        return plane * (4 + source % 4) + (1 - plane) * (source // 4 % 4)

    def first(self, work):
        mate = self.step(1, 0, 0)
        self.arrive(mate)
        self.sides(1)
        work([self.me, mate])
        for kind in (0, 1):
            for near in (1, 3):
                source = self.step(kind, near, 0)
                self.arrive(source)
                self.copy(source, self.step(kind, 4 - near, 0, True), 1 if near == 1 else 0, kind).start()
            if kind == 0:
                self.fan(1, 0)
        for kind in (0, 1):
            for near in (1, 3):
                self.fan(kind, near)
        work([self.step(kind, near, 0) for kind in (0, 1) for near in (1, 3)])
        for kind in (0, 1):
            self.arrive(self.step(kind, 2, 0), True)
            self.fan(kind, 2)
        work([self.step(kind, 2, 0) for kind in (0, 1)])

    def onward(self, near):
        for kind in (0, 1):
            for far in (1, 3):
                source = self.step(kind, near, far)
                self.arrive(source)
                self.copy(source, self.step(kind, 0, 4 - far, True), 1 if far == 1 else 0, 2 + kind * 4 + near).start()

    def last(self):
        @pl.loop(0, 4)
        def _(near):
            for kind in (0, 1):
                self.arrive(self.step(kind, near, 2), True)

    def finish(self):
        peer = ring(1 - self.z, self.x, self.y)

        @pl.loop(0, 21)
        def _(n):
            self.copy(self.me, peer, None, n).wait_send()

        @pl.loop(0, 10)
        def _(n):
            for half in (0, 1):
                self.copy(self.me, peer, half, n).wait_send()


def lay_out(spec_ref, own_ref, tmpl_ref, seg_ref, blk_ref, tm_ref, held, tn, nat, listed, me):
    listed[...] = jnp.zeros_like(listed)
    for v, ref in enumerate((own_ref, tmpl_ref, seg_ref, blk_ref)):
        listed[pl.ds(v, 1), pl.ds(0, 64)] = ref[...].astype(F32)
    held[me, pl.ds(128, 16), :] = listed[...].astype(BF)
    for p in range(2):
        for d in range(2):
            value = spec_ref[p, d].astype(F32)
            for c in range(32):
                nat[p, d, pl.ds(c, 2, stride=32), :] = value[:, 128 * c : 128 * c + 128]
    for p in range(2):
        for d in range(2):
            held[me, pl.ds(p * ROWS_A + 64 * d, 64), :] = nat[p, d, pl.ds(0, 64), :].astype(BF)


def prepare(tm_ref, bounds_ref, tmf, tn, nat, itp, masks, pick, weight):
    lane = iota((16, 128), 1)
    sub = iota((16, 128), 0)
    quarter, chunk = lane // 32, lane % 32
    cls = sub % 3
    natural = iota((32, 128), 0) * 128 + iota((32, 128), 1)
    freq = iota((16, F), 1)
    h0 = tm_ref[0].astype(F32)
    h1 = tm_ref[1].astype(F32)
    tmf[0] = h0
    tmf[1] = h1
    for p in range(2):
        for h in range(2):
            for c in range(32):
                nat[p, h, pl.ds(c, 8, stride=32), :] = tmf[p, pl.ds(8 * h, 8), pl.ds(128 * c, 128)]
            for m in range(8):
                tn[p, 8 * h + m] = nat[p, h, pl.ds(32 * m, 32), :].astype(BF)
    energy = h0 * h0 + h1 * h1
    rows16 = iota((16, 1), 0)

    def column(l):
        col = jnp.zeros((16, 1), I32)
        for m in range(NT):
            col = jnp.where(rows16 == m, bounds_ref[m, l], col)
        return col

    edges = [jnp.zeros((16, 1), I32)] + [column(l) for l in range(15)] + [jnp.full((16, 1), F, I32)]
    total = jnp.zeros((16, 1), F32)
    powers = jnp.zeros((16, 128), F32)
    for l in range(NBINS):
        inside = (freq >= edges[l]) & (freq < edges[l + 1])
        band = jnp.sum(jnp.where(inside, energy, 0.0), axis=1, keepdims=True) + EPSILON
        total = total + band
        powers = jnp.where(lane == l, band, powers)
    inverse = jnp.broadcast_to(1.0 / total, (16, 128))
    itp[...] = inverse
    none = jnp.zeros((16, 96), F32)
    short = iota((16, 96), 0)
    sums = jnp.concatenate([jnp.where(short == 0, 1.0, none), jnp.where(short == 1, 1.0, none)], 1)
    for m in range(NT):
        low = jnp.zeros((16, 128), I32)
        high = jnp.full((16, 128), F, I32)
        index = jnp.zeros((32, 128), I32)
        for l in range(15):
            edge = bounds_ref[m, l]
            low = jnp.where(sub == l + 1, edge, low)
            high = jnp.where(sub == l, edge, high)
            index = index + jnp.where(natural >= edge, 1, 0)
        touch = (cls == quarter) & (low < 128 * chunk + 128) & (high > 128 * chunk)
        touch = jnp.where(touch, 1.0, 0.0)[:, :96]
        pick[m] = jnp.concatenate(
            [jnp.concatenate([touch, none], 1), jnp.concatenate([none, touch], 1), sums], 0
        ).astype(BF)
        own = jnp.where(sub == lane, jnp.broadcast_to(powers[m : m + 1], (16, 128)), 0.0)
        own = jnp.sum(own, axis=1, keepdims=True)
        bands = jnp.broadcast_to(1.0 / own, (16, 128))
        whole = jnp.where(sub < 2, -jnp.broadcast_to(inverse[m : m + 1], (16, 128)), 0.0)
        weight[m] = jnp.concatenate([bands, bands, whole], 0) * (1.0 / (2.0 * (NBINS - 1)))
        index = index - 3 * ((index * 11) >> 5)
        for q in range(3):
            masks[m, q] = jnp.where(index == q, 1.0, 0.0).astype(BF)


def turn(held, rot_ref, turned, nat, source, k):
    rc, rs = rot_ref[0], rot_ref[1]
    for q in range(4):
        re = held[source, pl.ds(32 * q, 32), :].astype(F32)
        im = held[source, pl.ds(ROWS_A + 32 * q, 32), :].astype(F32)
        tr = re * rc - im * rs
        ti = re * rs + im * rc
        turned[k, q] = tr.astype(BF)
        turned[k, 4 + q] = ti.astype(BF)
        nat[0, q, pl.ds(pl.multiple_of(k * 32, 32), 32), :] = tr
        nat[1, q, pl.ds(pl.multiple_of(k * 32, 32), 32), :] = ti


def spread(nat, sre, sim):
    for q in range(4):
        for c in range(32):
            sre[pl.ds(8 * q, 8), pl.ds(c * 128, 128)] = nat[0, q, pl.ds(c, 8, stride=32), :]
            sim[pl.ds(8 * q, 8), pl.ds(c * 128, 128)] = nat[1, q, pl.ds(c, 8, stride=32), :]


def requests(place, held, wanted, meta, sem, sources):
    shard = place.me.astype(F32)
    tiles = [held[source, pl.ds(128, 16), :].astype(F32) for source in sources]
    tiles = tiles + tiles[:1] * (8 - len(tiles))
    rows = [jnp.concatenate([t[v : v + 1] for t in tiles], 0) for v in range(4)]
    lane = iota((8, 128), 1)
    hit = (rows[0] == shard) & (lane < 64)
    before = jnp.where(iota((128, 128), 0) < iota((128, 128), 1), 1.0, 0.0).astype(BF)
    rank = jnp.dot(jnp.where(hit, 1.0, 0.0).astype(BF), before, preferred_element_type=F32)
    terms = [jnp.where(hit & (rank == float(k)), rows[v + 1], 0.0) for v in range(3) for k in range(4)]
    sums = jnp.dot(jnp.concatenate(terms, 0).astype(BF), jnp.ones((128, 128), BF), preferred_element_type=F32)
    table = jnp.zeros((8, 128), F32)
    for n in range(12):
        table = jnp.where(lane == n, sums[8 * n : 8 * n + 8], table)
    wanted[...] = table.astype(I32)
    copy = pltpu.make_async_copy(wanted, meta, sem)
    copy.start()
    return copy


def veto(w0_ref, far_ref, tn, meta, turned, masks, pick, weight, chi, row, slot, source):
    fc, fs = far_ref[0], far_ref[1]
    rows = []
    at = []
    for k in range(4):
        m = jnp.clip(meta[row, k], 0, NT - 1)
        r = jnp.clip(meta[row, 4 + k], 0, 1)
        blk = jnp.clip(meta[row, 8 + k], 0, 1)
        at.append((m, blk))
        h0, h1 = tn[0, m], tn[1, m]
        sign = (2 * blk - 1).astype(F32).astype(BF)
        for d in range(2):
            re = turned[slot, 2 * d + r]
            im = turned[slot, 4 + 2 * d + r]
            xr = re * h0 + im * h1
            xi = (im * h0 - re * h1) * sign
            for q in range(3):
                mask = masks[m, q]
                rows.append(jnp.concatenate([xr * mask, xi * mask], 1))
    part = jnp.dot(jnp.concatenate(rows, 0), w0_ref[...], preferred_element_type=F32).astype(BF)
    lines = []
    for k in range(4):
        m, blk = at[k]
        turns = []
        for q in range(6):
            base = k * 192 + 32 * q
            ur = part[base : base + 32, :128]
            ui = part[base : base + 32, 128:]
            turns.append(jnp.concatenate([ur * fc - ui * fs, ur * fs + ui * fc], 1))
        bands = jnp.dot(pick[m], jnp.concatenate(turns, 0), preferred_element_type=F32)
        s = bands[:, :128] * bands[:, :128] + bands[:, 128:] * bands[:, 128:]
        lines.append((blk, jnp.sum(s * weight[m], axis=0, keepdims=True)))
    value = jnp.concatenate([line for _, line in lines] * 2, 0)
    back = jnp.take_along_axis(value, 127 - iota((8, 128), 1), axis=1)
    sub = iota((8, 128), 0) % 4
    late = jnp.zeros((8, 128), I32)
    for k in range(4):
        late = jnp.where(sub == k, lines[k][0], late)
    chi[source // 4, source % 4] = jnp.where(late == 1, value, back)


def filters(place, table_ref, tmf, itp, sre, sim, lhs, snr_ref, peak, member, first):
    for n in range(4):
        for k in range(F // 256):
            cut = pl.ds(k * 256, 256)
            h0 = tmf[0, pl.ds(first + n, 1), cut]
            h1 = tmf[1, pl.ds(first + n, 1), cut]
            re = sre[:, cut]
            im = sim[:, cut]
            lhs[pl.ds(64 * n, 32), cut] = (re * h0 + im * h1).astype(BF)
            lhs[pl.ds(64 * n + 32, 32), cut] = (im * h0 - re * h1).astype(BF)
    acc = jnp.dot(lhs[...], table_ref[...], preferred_element_type=F32)
    back = 127 - iota((16, 128), 1)
    bases = [member(k) * 4 for k in range(8)]
    for n in range(4):
        a = acc[64 * n : 64 * n + 32, :128]
        d = acc[64 * n : 64 * n + 32, 128:]
        c = acc[64 * n + 32 : 64 * n + 64, :128]
        b = acc[64 * n + 32 : 64 * n + 64, 128:]
        plus = (a - b) * (a - b) + (c + d) * (c + d)
        minus = (a + b) * (a + b) + (c - d) * (c - d)
        scale = itp[pl.ds(first + n, 1), :]
        plus = (plus[:16] + plus[16:]) * scale
        minus = (minus[:16] + minus[16:]) * scale
        top = jnp.maximum(plus, minus)
        top = jnp.maximum(top[:8], top[8:])
        peak[first + n] = jnp.maximum(peak[first + n], top)
        minus = jnp.take_along_axis(minus, back, axis=1)
        for half, value in enumerate((minus, plus)):
            for r in range(2):
                to = 2 * half + r
                for k in range(8):
                    line = value[8 * r + k : 8 * r + k + 1]
                    snr_ref[first + n, pl.ds(bases[k] + to, 1), :] = line


def kernel(
    spec_in, own_in, tmpl_in, seg_in, blk_in, tm_in, bounds_in, rot_in, w0_in, far_in, table_in,
    snr_ref, loud_ref, out_ref,
    spec_ref, own_ref, tmpl_ref, seg_ref, blk_ref, tm_ref, bounds_ref, rot_ref, w0_ref, far_ref, table_ref,
    held, listed, tmf, tn, itp, masks, pick, weight, turned, nat, sre, sim, lhs, peak, wanted, meta,
    chi, over, slots, tops, peaks,
    full_sem, half_sem, recv_sem, meta_sem, chi_send, chi_recv, pair_send, pair_recv, in_sem,
):
    place = Torus(held, full_sem, half_sem, recv_sem)
    me, seg = place.me, place.seg
    barrier = pltpu.get_barrier_semaphore()
    given = (spec_in, own_in, tmpl_in, seg_in, blk_in, tm_in, bounds_in, rot_in, w0_in, far_in, table_in)
    kept = (spec_ref, own_ref, tmpl_ref, seg_ref, blk_ref, tm_ref, bounds_ref, rot_ref, w0_ref, far_ref, table_ref)
    inputs = [pltpu.make_async_copy(a, b, in_sem.at[n]) for n, (a, b) in enumerate(zip(given, kept))]
    for copy in inputs:
        copy.start()

    z, x, y = place.z, place.x, place.y
    plane = me // 4
    friends = [(((plane + j) % 8) * 4 + y, seg) for j in range(1, 8)]
    friends += [(ring(z, x, y + j), seg) for j in range(1, 4)]
    friends += [(me, (seg + j) % 4) for j in range(1, 4)]
    for friend in friends:
        pl.semaphore_signal(barrier, inc=1, device_id=friend, device_id_type=MESH)
    for copy in inputs[:5]:
        copy.wait()
    lay_out(spec_ref, own_ref, tmpl_ref, seg_ref, blk_ref, tm_ref, held, tn, nat, listed, me)
    pl.semaphore_wait(barrier, 13)
    place.begin()
    for copy in inputs[5:]:
        copy.wait()
    prepare(tm_ref, bounds_ref, tmf, tn, nat, itp, masks, pick, weight)
    peak[...] = jnp.zeros_like(peak)

    def work(sources):
        asked = requests(place, held, wanted, meta, meta_sem, sources)
        for source in sources:
            turn(held, rot_ref, turned, nat, source, place.place_of(source))
        asked.wait()
        for row, source in enumerate(sources):
            veto(w0_ref, far_ref, tn, meta, turned, masks, pick, weight, chi, row, place.place_of(source), source)

    def serve(member):
        asked = requests(place, held, wanted, meta, meta_sem, [member(k) for k in range(8)])

        @pl.loop(0, 8)
        def _(k):
            turn(held, rot_ref, turned, nat, member(k), k)

        asked.wait()

        @pl.loop(0, 2)
        def _(part):
            for n in range(4):
                slot = part * 4 + n
                veto(w0_ref, far_ref, tn, meta, turned, masks, pick, weight, chi, slot, slot, member(slot))

    def scan(member, between):
        spread(nat, sre, sim)

        @pl.loop(0, 4)
        def _(step):
            filters(place, table_ref, tmf, itp, sre, sim, lhs, snr_ref, peak, member, step * 4)
            between(step)

    def result(axis, j):
        if axis == 0:
            to = (plane + j) % 8
            src, dst, peer = chi.at[to], over.at[plane], to * 4 + y
        else:
            src, dst, peer = over.at[:, (y + j) % 4], slots.at[y], ring(z, x, y + j)
        return pltpu.make_async_remote_copy(
            src_ref=src,
            dst_ref=dst,
            send_sem=chi_send.at[axis, j],
            recv_sem=chi_recv.at[axis, j],
            device_id=(peer, seg),
            device_id_type=MESH,
        )

    place.first(work)

    def pass_on(step):
        @pl.when(step == 2)
        def _():
            place.onward(0)

    scan(place.early, pass_on)
    place.onward(1)

    @pl.loop(0, 2)
    def _(part):
        serve(lambda k: place.beside(part, k))

        @pl.when(part == 0)
        def _():
            place.onward(3)

        def pass_more(step):
            @pl.when((step == 2) & (part == 0))
            def _():
                place.onward(2)

        scan(lambda k: place.beside(part, k), pass_more)

    place.last()
    serve(place.across)
    for j in range(1, 8):
        result(0, j).start()
    over[pl.ds(plane, 1)] = chi[pl.ds(plane, 1)]

    def homeward(step):
        @pl.when(step == 2)
        def _():
            for j in range(1, 8):
                result(0, j).wait()
            for j in (1, 2, 3):
                result(1, j).start()
            for n in range(8):
                slots[y, n] = over[n, y]

    scan(place.across, homeward)
    tops[...] = jnp.concatenate([jnp.max(peak[m], axis=0, keepdims=True) for m in range(NT)], 0)
    pairs = [
        pltpu.make_async_remote_copy(
            src_ref=tops,
            dst_ref=peaks.at[j],
            send_sem=pair_send.at[j],
            recv_sem=pair_recv.at[j],
            device_id=(me, (seg + j) % 4),
            device_id_type=MESH,
        )
        for j in range(1, 4)
    ]
    for copy in pairs:
        copy.start()
    place.finish()
    for j in (1, 2, 3):
        result(1, j).wait()
    i, j = iota((64, 64), 0), iota((64, 64), 1)
    across = own_ref[...]
    owner = jnp.sum(jnp.where(i == j, across, 0), axis=1, keepdims=True)
    rank = jnp.sum(jnp.where((j < i) & (across == owner), 1, 0), axis=1, keepdims=True)
    where = owner % 4 * 8 + owner // 4
    choose = jnp.where(iota((64, 256), 1) == where * 8 + rank, 1.0, 0.0)
    out_ref[...] = jnp.dot(
        choose, slots[...].reshape(256, 128), preferred_element_type=F32, precision=lax.Precision.HIGHEST
    )
    for copy in pairs:
        copy.wait()
    top = jnp.maximum(jnp.maximum(tops[...], peaks[1]), jnp.maximum(peaks[2], peaks[3]))
    top = jnp.max(top, axis=1, keepdims=True)
    loud = jnp.max(jnp.where(iota((NT, 128), 0) == iota((NT, 128), 1), top, 0.0), axis=0, keepdims=True)
    loud_ref[...] = loud[:, :NT]


def handed_kernel(*refs):
    for n in range(3):
        refs[n + 3][...] = refs[n][...]


def handed(*arrays):
    vmem = pl.BlockSpec(memory_space=pltpu.VMEM)
    return pl.pallas_call(
        handed_kernel,
        out_shape=tuple(jax.ShapeDtypeStruct(a.shape, a.dtype) for a in arrays),
        in_specs=[vmem] * 3,
        out_specs=(vmem,) * 3,
        name="handed",
    )(*arrays)


def body(
    spectra, templates, bounds, trigger_owner, trigger_template, trigger_segment, trigger_block
):
    vmem = pl.BlockSpec(memory_space=pltpu.VMEM)
    dma = pltpu.SemaphoreType.DMA
    wave, rot, w0, far = tables()
    snr, loud, chisq = pl.pallas_call(
        kernel,
        out_shape=(
            jax.ShapeDtypeStruct((NT, 128, 128), F32),
            jax.ShapeDtypeStruct((1, NT), F32),
            jax.ShapeDtypeStruct((64, 128), F32),
        ),
        in_specs=[pl.BlockSpec(memory_space=pltpu.HBM)] * 11,
        out_specs=(vmem, vmem, vmem),
        scratch_shapes=[
            pltpu.VMEM((2, 2, 2, F), BF),
            pltpu.VMEM((1, 64), I32),
            pltpu.VMEM((1, 64), I32),
            pltpu.VMEM((1, 64), I32),
            pltpu.VMEM((1, 64), I32),
            pltpu.VMEM((2, NT, F), BF),
            pltpu.SMEM((NT, 15), I32),
            pltpu.VMEM((2, 32, 128), F32),
            pltpu.VMEM((256, 256), BF),
            pltpu.VMEM((2, 32, 128), BF),
            pltpu.VMEM((F, 256), BF),
            pltpu.VMEM((32, ROWS, 128), BF),
            pltpu.VMEM((16, 128), F32),
            pltpu.VMEM((2, NT, F), F32),
            pltpu.VMEM((2, NT, 32, 128), BF),
            pltpu.VMEM((NT, 128), F32),
            pltpu.VMEM((NT, 3, 32, 128), BF),
            pltpu.VMEM((NT, 48, 192), BF),
            pltpu.VMEM((NT, 48, 128), F32),
            pltpu.VMEM((8, 8, 32, 128), BF),
            pltpu.VMEM((2, 4, 288, 128), F32),
            pltpu.VMEM((32, F), F32),
            pltpu.VMEM((32, F), F32),
            pltpu.VMEM((256, F), BF),
            pltpu.VMEM((NT, 8, 128), F32),
            pltpu.VMEM((8, 128), I32),
            pltpu.SMEM((8, 128), I32),
            pltpu.VMEM((8, 4, 8, 128), F32),
            pltpu.VMEM((8, 4, 8, 128), F32),
            pltpu.VMEM((4, 8, 8, 128), F32),
            pltpu.VMEM((NT, 128), F32),
            pltpu.VMEM((4, NT, 128), F32),
            dma((21,)),
            dma((2, 10)),
            dma((2, 32)),
            dma,
            dma((2, 8)),
            dma((2, 8)),
            dma((4,)),
            dma((4,)),
            dma((11,)),
        ],
        compiler_params=pltpu.CompilerParams(
            collective_id=0, has_side_effects=True, vmem_limit_bytes=62 * 1024 * 1024
        ),
        name="search",
    )(
        spectra.reshape(2, 2, 2, F),
        trigger_owner.reshape(1, 64),
        trigger_template.reshape(1, 64),
        trigger_segment.reshape(1, 64),
        trigger_block.reshape(1, 64),
        templates,
        bounds,
        rot,
        w0,
        far,
        wave,
    )
    snr, loud, chisq = handed(snr, loud, chisq)
    snr = snr.reshape(NT, 32, 2, 2, 128).transpose(0, 1, 3, 2, 4).reshape(NT, 32, 2, 256)
    return snr, loud.reshape(NT), chisq


def solution(mesh):
    in_specs = (
        P(None, None, "tmpl", "seg", None),
        P(None, "tmpl", None),
        P("tmpl", None),
        P(("tmpl", "seg"), None),
        P(("tmpl", "seg")),
        P(("tmpl", "seg")),
        P(("tmpl", "seg")),
    )
    out_specs = (P("tmpl", None, "seg", None), P("tmpl"), P(("tmpl", "seg"), None))
    return jax.shard_map(body, mesh=mesh, in_specs=in_specs, out_specs=out_specs, check_vma=False)
```

```python
import math

import jax
import jax.numpy as jnp
import numpy as np
from jax import lax
from jax.experimental import pallas as pl
from jax.experimental.pallas import tpu as pltpu
from jax.sharding import PartitionSpec as P

F = 4096
NT = 16
NBINS = 16
EPSILON = 1e-06
BF = jnp.bfloat16
F32 = jnp.float32
I32 = jnp.int32
MESH = pl.DeviceIdType.MESH
ROWS_A = 144
ROWS = 272


def tables():
    step = 2.0 * math.pi / 4096.0
    phi = np.arange(4096, dtype=np.float64) - 2048.0
    half = np.arange(128, dtype=np.float64) + 0.5
    ang = step * phi[:, None] * half[None, :]
    main = np.concatenate([np.cos(ang), np.sin(ang)], 1)
    turn = (step * 127.5 * phi).reshape(32, 128)
    rot = np.stack([np.cos(turn), np.sin(turn)])
    near = step * np.arange(128.0)[:, None] * half[None, :]
    w0 = np.concatenate(
        [
            np.concatenate([np.cos(near), np.sin(near)], 1),
            np.concatenate([-np.sin(near), np.cos(near)], 1),
        ],
        0,
    )
    far = step * (128.0 * np.arange(32.0) - 2048.0)[:, None] * half[None, :]
    far = np.stack([np.cos(far), np.sin(far)])
    return (
        jnp.asarray(main, F32).astype(BF),
        jnp.asarray(rot, F32),
        jnp.asarray(w0, F32).astype(BF),
        jnp.asarray(far, F32).astype(BF),
    )


def iota(shape, dim):
    return lax.broadcasted_iota(I32, shape, dim)


def ring(zz, xx, yy):
    return zz * 16 + xx % 4 * 4 + yy % 4


class Torus:
    def __init__(self, held, full_sem, half_sem, recv_sem):
        self.me = lax.axis_index("tmpl")
        self.seg = lax.axis_index("seg")
        self.z, self.x, self.y = self.me // 16, self.me // 4 % 4, self.me % 4
        self.held, self.full_sem, self.half_sem, self.recv_sem = held, full_sem, half_sem, recv_sem

    def step(self, kind, near, far, here=False):
        plane = self.z * (1 - kind) + (1 - self.z) * kind
        xx = self.x + near * (1 - plane) + far * plane
        yy = self.y + near * plane + far * (1 - plane)
        return ring(self.z if here else plane, xx, yy)

    def early(self, k):
        plane, at = k // 4, k % 4
        return (1 - plane) * (at * 4 + self.y) + plane * (16 + self.x * 4 + at)

    def beside(self, part, k):
        one = k // 2 % 2
        return self.step(k // 4, part * (3 - one) + (1 - part) * one, 1 + 2 * (k % 2))

    def across(self, k):
        return self.step(k // 4, k % 4, 2)

    def copy(self, source, peer, half, sem):
        if half is None:
            view, recv, send = self.held.at[source], self.recv_sem.at[0, source], self.full_sem.at[sem]
        else:
            cut = pl.ds(0, ROWS_A) if half == 0 else pl.ds(ROWS_A, ROWS - ROWS_A)
            view, recv, send = self.held.at[source, cut], self.recv_sem.at[half, source], self.half_sem.at[half, sem]
        return pltpu.make_async_remote_copy(
            src_ref=view, dst_ref=view, send_sem=send, recv_sem=recv, device_id=(peer, self.seg), device_id_type=MESH
        )

    def arrive(self, source, halves=False):
        peer = ring(1 - self.z, self.x, self.y)
        for half in (0, 1) if halves else (None,):
            self.copy(source, peer, half, 0).wait_recv()

    def fan(self, kind, near):
        source = self.step(kind, near, 0)
        for n, far in enumerate((1, 3)):
            self.copy(source, self.step(kind, 0, far, True), None, 5 + kind * 8 + near * 2 + n).start()

    def sides(self, kind):
        source = self.step(kind, 0, 0)
        for n, near in enumerate((1, 3)):
            self.copy(source, self.step(kind, near, 0, True), None, 1 + kind * 2 + n).start()

    def begin(self):
        mate = ring(1 - self.z, self.x, self.y)
        self.copy(self.me, mate, None, 0).start()
        self.sides(0)
        self.fan(0, 0)

    def place_of(self, source):
        plane = source // 16
        return plane * (4 + source % 4) + (1 - plane) * (source // 4 % 4)

    def first(self, work):
        mate = self.step(1, 0, 0)
        self.arrive(mate)
        self.sides(1)
        work([self.me, mate])
        for kind in (0, 1):
            for near in (1, 3):
                source = self.step(kind, near, 0)
                self.arrive(source)
                self.copy(source, self.step(kind, 4 - near, 0, True), 1 if near == 1 else 0, kind).start()
            if kind == 0:
                self.fan(1, 0)
        for kind in (0, 1):
            for near in (1, 3):
                self.fan(kind, near)
        work([self.step(kind, near, 0) for kind in (0, 1) for near in (1, 3)])
        for kind in (0, 1):
            self.arrive(self.step(kind, 2, 0), True)
            self.fan(kind, 2)
        work([self.step(kind, 2, 0) for kind in (0, 1)])

    def onward(self, near):
        for kind in (0, 1):
            for far in (1, 3):
                source = self.step(kind, near, far)
                self.arrive(source)
                self.copy(source, self.step(kind, 0, 4 - far, True), 1 if far == 1 else 0, 2 + kind * 4 + near).start()

    def last(self):
        @pl.loop(0, 4)
        def _(near):
            for kind in (0, 1):
                self.arrive(self.step(kind, near, 2), True)

    def finish(self):
        peer = ring(1 - self.z, self.x, self.y)

        @pl.loop(0, 21)
        def _(n):
            self.copy(self.me, peer, None, n).wait_send()

        @pl.loop(0, 10)
        def _(n):
            for half in (0, 1):
                self.copy(self.me, peer, half, n).wait_send()


def lay_out(spec_ref, own_ref, tmpl_ref, seg_ref, blk_ref, tm_ref, held, tn, nat, listed, me):
    listed[...] = jnp.zeros_like(listed)
    for v, ref in enumerate((own_ref, tmpl_ref, seg_ref, blk_ref)):
        listed[pl.ds(v, 1), pl.ds(0, 64)] = ref[...].astype(F32)
    held[me, pl.ds(128, 16), :] = listed[...].astype(BF)
    for p in range(2):
        for d in range(2):
            value = spec_ref[p, d].astype(F32)
            for c in range(32):
                nat[p, d, pl.ds(c, 2, stride=32), :] = value[:, 128 * c : 128 * c + 128]
    for p in range(2):
        for d in range(2):
            held[me, pl.ds(p * ROWS_A + 64 * d, 64), :] = nat[p, d, pl.ds(0, 64), :].astype(BF)


def prepare(tm_ref, bounds_ref, tmf, tn, nat, itp, masks, pick, weight):
    lane = iota((16, 128), 1)
    sub = iota((16, 128), 0)
    quarter, chunk = lane // 32, lane % 32
    cls = sub % 3
    natural = iota((32, 128), 0) * 128 + iota((32, 128), 1)
    freq = iota((16, F), 1)
    h0 = tm_ref[0].astype(F32)
    h1 = tm_ref[1].astype(F32)
    tmf[0] = h0
    tmf[1] = h1
    for p in range(2):
        for h in range(2):
            for c in range(32):
                nat[p, h, pl.ds(c, 8, stride=32), :] = tmf[p, pl.ds(8 * h, 8), pl.ds(128 * c, 128)]
            for m in range(8):
                tn[p, 8 * h + m] = nat[p, h, pl.ds(32 * m, 32), :].astype(BF)
    energy = h0 * h0 + h1 * h1
    rows16 = iota((16, 1), 0)

    def column(l):
        col = jnp.zeros((16, 1), I32)
        for m in range(NT):
            col = jnp.where(rows16 == m, bounds_ref[m, l], col)
        return col

    edges = [jnp.zeros((16, 1), I32)] + [column(l) for l in range(15)] + [jnp.full((16, 1), F, I32)]
    total = jnp.zeros((16, 1), F32)
    powers = jnp.zeros((16, 128), F32)
    for l in range(NBINS):
        inside = (freq >= edges[l]) & (freq < edges[l + 1])
        band = jnp.sum(jnp.where(inside, energy, 0.0), axis=1, keepdims=True) + EPSILON
        total = total + band
        powers = jnp.where(lane == l, band, powers)
    inverse = jnp.broadcast_to(1.0 / total, (16, 128))
    itp[...] = inverse
    none = jnp.zeros((16, 96), F32)
    short = iota((16, 96), 0)
    sums = jnp.concatenate([jnp.where(short == 0, 1.0, none), jnp.where(short == 1, 1.0, none)], 1)
    for m in range(NT):
        low = jnp.zeros((16, 128), I32)
        high = jnp.full((16, 128), F, I32)
        index = jnp.zeros((32, 128), I32)
        for l in range(15):
            edge = bounds_ref[m, l]
            low = jnp.where(sub == l + 1, edge, low)
            high = jnp.where(sub == l, edge, high)
            index = index + jnp.where(natural >= edge, 1, 0)
        touch = (cls == quarter) & (low < 128 * chunk + 128) & (high > 128 * chunk)
        touch = jnp.where(touch, 1.0, 0.0)[:, :96]
        pick[m] = jnp.concatenate(
            [jnp.concatenate([touch, none], 1), jnp.concatenate([none, touch], 1), sums], 0
        ).astype(BF)
        own = jnp.where(sub == lane, jnp.broadcast_to(powers[m : m + 1], (16, 128)), 0.0)
        own = jnp.sum(own, axis=1, keepdims=True)
        bands = jnp.broadcast_to(1.0 / own, (16, 128))
        whole = jnp.where(sub < 2, -jnp.broadcast_to(inverse[m : m + 1], (16, 128)), 0.0)
        weight[m] = jnp.concatenate([bands, bands, whole], 0) * (1.0 / (2.0 * (NBINS - 1)))
        index = index - 3 * ((index * 11) >> 5)
        for q in range(3):
            masks[m, q] = jnp.where(index == q, 1.0, 0.0).astype(BF)


def turn(held, rot_ref, turned, nat, source, k):
    rc, rs = rot_ref[0], rot_ref[1]
    for q in range(4):
        re = held[source, pl.ds(32 * q, 32), :].astype(F32)
        im = held[source, pl.ds(ROWS_A + 32 * q, 32), :].astype(F32)
        tr = re * rc - im * rs
        ti = re * rs + im * rc
        turned[k, q] = tr.astype(BF)
        turned[k, 4 + q] = ti.astype(BF)
        nat[0, q, pl.ds(pl.multiple_of(k * 32, 32), 32), :] = tr
        nat[1, q, pl.ds(pl.multiple_of(k * 32, 32), 32), :] = ti


def spread(nat, sre, sim):
    for q in range(4):
        for c in range(32):
            sre[pl.ds(8 * q, 8), pl.ds(c * 128, 128)] = nat[0, q, pl.ds(c, 8, stride=32), :]
            sim[pl.ds(8 * q, 8), pl.ds(c * 128, 128)] = nat[1, q, pl.ds(c, 8, stride=32), :]


def requests(place, held, wanted, meta, sem, sources):
    shard = place.me.astype(F32)
    tiles = [held[source, pl.ds(128, 16), :].astype(F32) for source in sources]
    tiles = tiles + tiles[:1] * (8 - len(tiles))
    rows = [jnp.concatenate([t[v : v + 1] for t in tiles], 0) for v in range(4)]
    lane = iota((8, 128), 1)
    hit = (rows[0] == shard) & (lane < 64)
    before = jnp.where(iota((128, 128), 0) < iota((128, 128), 1), 1.0, 0.0).astype(BF)
    rank = jnp.dot(jnp.where(hit, 1.0, 0.0).astype(BF), before, preferred_element_type=F32)
    terms = [jnp.where(hit & (rank == float(k)), rows[v + 1], 0.0) for v in range(3) for k in range(4)]
    sums = jnp.dot(jnp.concatenate(terms, 0).astype(BF), jnp.ones((128, 128), BF), preferred_element_type=F32)
    table = jnp.zeros((8, 128), F32)
    for n in range(12):
        table = jnp.where(lane == n, sums[8 * n : 8 * n + 8], table)
    wanted[...] = table.astype(I32)
    copy = pltpu.make_async_copy(wanted, meta, sem)
    copy.start()
    return copy


def veto(w0_ref, far_ref, tn, meta, turned, masks, pick, weight, chi, row, slot, source):
    fc, fs = far_ref[0], far_ref[1]
    rows = []
    at = []
    for k in range(4):
        m = jnp.clip(meta[row, k], 0, NT - 1)
        r = jnp.clip(meta[row, 4 + k], 0, 1)
        blk = jnp.clip(meta[row, 8 + k], 0, 1)
        at.append((m, blk))
        h0, h1 = tn[0, m], tn[1, m]
        sign = (2 * blk - 1).astype(F32).astype(BF)
        for d in range(2):
            re = turned[slot, 2 * d + r]
            im = turned[slot, 4 + 2 * d + r]
            xr = re * h0 + im * h1
            xi = (im * h0 - re * h1) * sign
            for q in range(3):
                mask = masks[m, q]
                rows.append(jnp.concatenate([xr * mask, xi * mask], 1))
    part = jnp.dot(jnp.concatenate(rows, 0), w0_ref[...], preferred_element_type=F32).astype(BF)
    lines = []
    for k in range(4):
        m, blk = at[k]
        turns = []
        for q in range(6):
            base = k * 192 + 32 * q
            ur = part[base : base + 32, :128]
            ui = part[base : base + 32, 128:]
            turns.append(jnp.concatenate([ur * fc - ui * fs, ur * fs + ui * fc], 1))
        bands = jnp.dot(pick[m], jnp.concatenate(turns, 0), preferred_element_type=F32)
        s = bands[:, :128] * bands[:, :128] + bands[:, 128:] * bands[:, 128:]
        lines.append((blk, jnp.sum(s * weight[m], axis=0, keepdims=True)))
    value = jnp.concatenate([line for _, line in lines] * 2, 0)
    back = jnp.take_along_axis(value, 127 - iota((8, 128), 1), axis=1)
    sub = iota((8, 128), 0) % 4
    late = jnp.zeros((8, 128), I32)
    for k in range(4):
        late = jnp.where(sub == k, lines[k][0], late)
    chi[source // 4, source % 4] = jnp.where(late == 1, value, back)


def filters(place, table_ref, tmf, itp, sre, sim, lhs, snr_ref, peak, member, first):
    for n in range(4):
        for k in range(F // 256):
            cut = pl.ds(k * 256, 256)
            h0 = tmf[0, pl.ds(first + n, 1), cut]
            h1 = tmf[1, pl.ds(first + n, 1), cut]
            re = sre[:, cut]
            im = sim[:, cut]
            lhs[pl.ds(64 * n, 32), cut] = (re * h0 + im * h1).astype(BF)
            lhs[pl.ds(64 * n + 32, 32), cut] = (im * h0 - re * h1).astype(BF)
    acc = jnp.dot(lhs[...], table_ref[...], preferred_element_type=F32)
    back = 127 - iota((16, 128), 1)
    bases = [member(k) * 4 for k in range(8)]
    for n in range(4):
        a = acc[64 * n : 64 * n + 32, :128]
        d = acc[64 * n : 64 * n + 32, 128:]
        c = acc[64 * n + 32 : 64 * n + 64, :128]
        b = acc[64 * n + 32 : 64 * n + 64, 128:]
        plus = (a - b) * (a - b) + (c + d) * (c + d)
        minus = (a + b) * (a + b) + (c - d) * (c - d)
        scale = itp[pl.ds(first + n, 1), :]
        plus = (plus[:16] + plus[16:]) * scale
        minus = (minus[:16] + minus[16:]) * scale
        top = jnp.maximum(plus, minus)
        top = jnp.maximum(top[:8], top[8:])
        peak[first + n] = jnp.maximum(peak[first + n], top)
        minus = jnp.take_along_axis(minus, back, axis=1)
        for half, value in enumerate((minus, plus)):
            for r in range(2):
                to = 2 * half + r
                for k in range(8):
                    line = value[8 * r + k : 8 * r + k + 1]
                    snr_ref[first + n, pl.ds(bases[k] + to, 1), :] = line


def kernel(
    spec_in, own_in, tmpl_in, seg_in, blk_in, tm_in, bounds_in, rot_in, w0_in, far_in, table_in,
    snr_ref, loud_ref, out_ref,
    spec_ref, own_ref, tmpl_ref, seg_ref, blk_ref, tm_ref, bounds_ref, rot_ref, w0_ref, far_ref, table_ref,
    held, listed, tmf, tn, itp, masks, pick, weight, turned, nat, sre, sim, lhs, peak, wanted, meta,
    chi, over, slots, tops, peaks,
    full_sem, half_sem, recv_sem, meta_sem, chi_send, chi_recv, pair_send, pair_recv, in_sem,
):
    place = Torus(held, full_sem, half_sem, recv_sem)
    me, seg = place.me, place.seg
    barrier = pltpu.get_barrier_semaphore()
    given = (spec_in, own_in, tmpl_in, seg_in, blk_in, tm_in, bounds_in, rot_in, w0_in, far_in, table_in)
    kept = (spec_ref, own_ref, tmpl_ref, seg_ref, blk_ref, tm_ref, bounds_ref, rot_ref, w0_ref, far_ref, table_ref)
    inputs = [pltpu.make_async_copy(a, b, in_sem.at[n]) for n, (a, b) in enumerate(zip(given, kept))]
    for copy in inputs:
        copy.start()

    z, x, y = place.z, place.x, place.y
    plane = me // 4
    friends = [(((plane + j) % 8) * 4 + y, seg) for j in range(1, 8)]
    friends += [(ring(z, x, y + j), seg) for j in range(1, 4)]
    friends += [(me, (seg + j) % 4) for j in range(1, 4)]
    for friend in friends:
        pl.semaphore_signal(barrier, inc=1, device_id=friend, device_id_type=MESH)
    for copy in inputs[:5]:
        copy.wait()
    lay_out(spec_ref, own_ref, tmpl_ref, seg_ref, blk_ref, tm_ref, held, tn, nat, listed, me)
    pl.semaphore_wait(barrier, 13)
    place.begin()
    for copy in inputs[5:]:
        copy.wait()
    prepare(tm_ref, bounds_ref, tmf, tn, nat, itp, masks, pick, weight)
    peak[...] = jnp.zeros_like(peak)

    def work(sources):
        asked = requests(place, held, wanted, meta, meta_sem, sources)
        for source in sources:
            turn(held, rot_ref, turned, nat, source, place.place_of(source))
        asked.wait()
        for row, source in enumerate(sources):
            veto(w0_ref, far_ref, tn, meta, turned, masks, pick, weight, chi, row, place.place_of(source), source)

    def serve(member):
        asked = requests(place, held, wanted, meta, meta_sem, [member(k) for k in range(8)])
        for k in range(8):
            turn(held, rot_ref, turned, nat, member(k), k)
        asked.wait()
        for slot in range(8):
            veto(w0_ref, far_ref, tn, meta, turned, masks, pick, weight, chi, slot, slot, member(slot))

    def scan(member, between):
        spread(nat, sre, sim)

        @pl.loop(0, 4)
        def _(step):
            filters(place, table_ref, tmf, itp, sre, sim, lhs, snr_ref, peak, member, step * 4)
            between(step)

    def result(axis, j):
        if axis == 0:
            to = (plane + j) % 8
            src, dst, peer = chi.at[to], over.at[plane], to * 4 + y
        else:
            src, dst, peer = over.at[:, (y + j) % 4], slots.at[y], ring(z, x, y + j)
        return pltpu.make_async_remote_copy(
            src_ref=src,
            dst_ref=dst,
            send_sem=chi_send.at[axis, j],
            recv_sem=chi_recv.at[axis, j],
            device_id=(peer, seg),
            device_id_type=MESH,
        )

    place.first(work)

    def pass_on(step):
        @pl.when(step == 2)
        def _():
            place.onward(0)

    scan(place.early, pass_on)
    place.onward(1)

    @pl.loop(0, 2)
    def _(part):
        serve(lambda k: place.beside(part, k))

        @pl.when(part == 0)
        def _():
            place.onward(3)

        def pass_more(step):
            @pl.when((step == 2) & (part == 0))
            def _():
                place.onward(2)

        scan(lambda k: place.beside(part, k), pass_more)

    place.last()
    serve(place.across)
    for j in range(1, 8):
        result(0, j).start()
    over[pl.ds(plane, 1)] = chi[pl.ds(plane, 1)]

    def homeward(step):
        @pl.when(step == 2)
        def _():
            for j in range(1, 8):
                result(0, j).wait()
            for j in (1, 2, 3):
                result(1, j).start()
            for n in range(8):
                slots[y, n] = over[n, y]

    scan(place.across, homeward)
    tops[...] = jnp.concatenate([jnp.max(peak[m], axis=0, keepdims=True) for m in range(NT)], 0)
    pairs = [
        pltpu.make_async_remote_copy(
            src_ref=tops,
            dst_ref=peaks.at[j],
            send_sem=pair_send.at[j],
            recv_sem=pair_recv.at[j],
            device_id=(me, (seg + j) % 4),
            device_id_type=MESH,
        )
        for j in range(1, 4)
    ]
    for copy in pairs:
        copy.start()
    place.finish()
    for j in (1, 2, 3):
        result(1, j).wait()
    i, j = iota((64, 64), 0), iota((64, 64), 1)
    across = own_ref[...]
    owner = jnp.sum(jnp.where(i == j, across, 0), axis=1, keepdims=True)
    rank = jnp.sum(jnp.where((j < i) & (across == owner), 1, 0), axis=1, keepdims=True)
    where = owner % 4 * 8 + owner // 4
    choose = jnp.where(iota((64, 256), 1) == where * 8 + rank, 1.0, 0.0)
    out_ref[...] = jnp.dot(
        choose, slots[...].reshape(256, 128), preferred_element_type=F32, precision=lax.Precision.HIGHEST
    )
    for copy in pairs:
        copy.wait()
    top = jnp.maximum(jnp.maximum(tops[...], peaks[1]), jnp.maximum(peaks[2], peaks[3]))
    top = jnp.max(top, axis=1, keepdims=True)
    loud = jnp.max(jnp.where(iota((NT, 128), 0) == iota((NT, 128), 1), top, 0.0), axis=0, keepdims=True)
    loud_ref[...] = loud[:, :NT]


def handed_kernel(*refs):
    for n in range(3):
        refs[n + 3][...] = refs[n][...]


def handed(*arrays):
    vmem = pl.BlockSpec(memory_space=pltpu.VMEM)
    return pl.pallas_call(
        handed_kernel,
        out_shape=tuple(jax.ShapeDtypeStruct(a.shape, a.dtype) for a in arrays),
        in_specs=[vmem] * 3,
        out_specs=(vmem,) * 3,
        name="handed",
    )(*arrays)


def body(
    spectra, templates, bounds, trigger_owner, trigger_template, trigger_segment, trigger_block
):
    vmem = pl.BlockSpec(memory_space=pltpu.VMEM)
    dma = pltpu.SemaphoreType.DMA
    wave, rot, w0, far = tables()
    snr, loud, chisq = pl.pallas_call(
        kernel,
        out_shape=(
            jax.ShapeDtypeStruct((NT, 128, 128), F32),
            jax.ShapeDtypeStruct((1, NT), F32),
            jax.ShapeDtypeStruct((64, 128), F32),
        ),
        in_specs=[pl.BlockSpec(memory_space=pltpu.HBM)] * 11,
        out_specs=(vmem, vmem, vmem),
        scratch_shapes=[
            pltpu.VMEM((2, 2, 2, F), BF),
            pltpu.VMEM((1, 64), I32),
            pltpu.VMEM((1, 64), I32),
            pltpu.VMEM((1, 64), I32),
            pltpu.VMEM((1, 64), I32),
            pltpu.VMEM((2, NT, F), BF),
            pltpu.SMEM((NT, 15), I32),
            pltpu.VMEM((2, 32, 128), F32),
            pltpu.VMEM((256, 256), BF),
            pltpu.VMEM((2, 32, 128), BF),
            pltpu.VMEM((F, 256), BF),
            pltpu.VMEM((32, ROWS, 128), BF),
            pltpu.VMEM((16, 128), F32),
            pltpu.VMEM((2, NT, F), F32),
            pltpu.VMEM((2, NT, 32, 128), BF),
            pltpu.VMEM((NT, 128), F32),
            pltpu.VMEM((NT, 3, 32, 128), BF),
            pltpu.VMEM((NT, 48, 192), BF),
            pltpu.VMEM((NT, 48, 128), F32),
            pltpu.VMEM((8, 8, 32, 128), BF),
            pltpu.VMEM((2, 4, 288, 128), F32),
            pltpu.VMEM((32, F), F32),
            pltpu.VMEM((32, F), F32),
            pltpu.VMEM((256, F), BF),
            pltpu.VMEM((NT, 8, 128), F32),
            pltpu.VMEM((8, 128), I32),
            pltpu.SMEM((8, 128), I32),
            pltpu.VMEM((8, 4, 8, 128), F32),
            pltpu.VMEM((8, 4, 8, 128), F32),
            pltpu.VMEM((4, 8, 8, 128), F32),
            pltpu.VMEM((NT, 128), F32),
            pltpu.VMEM((4, NT, 128), F32),
            dma((21,)),
            dma((2, 10)),
            dma((2, 32)),
            dma,
            dma((2, 8)),
            dma((2, 8)),
            dma((4,)),
            dma((4,)),
            dma((11,)),
        ],
        compiler_params=pltpu.CompilerParams(
            collective_id=0, has_side_effects=True, vmem_limit_bytes=62 * 1024 * 1024
        ),
        name="search",
    )(
        spectra.reshape(2, 2, 2, F),
        trigger_owner.reshape(1, 64),
        trigger_template.reshape(1, 64),
        trigger_segment.reshape(1, 64),
        trigger_block.reshape(1, 64),
        templates,
        bounds,
        rot,
        w0,
        far,
        wave,
    )
    snr, loud, chisq = handed(snr, loud, chisq)
    snr = snr.reshape(NT, 32, 2, 2, 128).transpose(0, 1, 3, 2, 4).reshape(NT, 32, 2, 256)
    return snr, loud.reshape(NT), chisq


def solution(mesh):
    in_specs = (
        P(None, None, "tmpl", "seg", None),
        P(None, "tmpl", None),
        P("tmpl", None),
        P(("tmpl", "seg"), None),
        P(("tmpl", "seg")),
        P(("tmpl", "seg")),
        P(("tmpl", "seg")),
    )
    out_specs = (P("tmpl", None, "seg", None), P("tmpl"), P(("tmpl", "seg"), None))
    return jax.shard_map(body, mesh=mesh, in_specs=in_specs, out_specs=out_specs, check_vma=False)
```
